32 devices in a mesh: groups: 2 (over y), series: 2 (over core), tm: 8 (over z, x).
Axes of the slice: x: 2, y: 2, z: 4, core: 2. Of those that a mesh axis runs over, the one named last changes fastest.
Arguments:
- history: bfloat16 [4, 8192, 512], P(('groups', 'series'), 'tm'), parts along dimension 0, may hold values from -6 to 6
- convolution_taps: float32 [2, 3, 512], replicated, may hold values from -3 to 3
- norm_gain_pair: float32 [2, 512], replicated, may hold values from 0.25 to 1.75
- up_projection: bfloat16 [2, 512, 1024], replicated, may hold values from -0.25 to 0.25
- down_projection: bfloat16 [2, 1024, 512], replicated, may hold values from -0.1875 to 0.1875
- w_kv: bfloat16 [512, 1024], replicated, may hold values from -0.25 to 0.25
- readout_matrix: bfloat16 [512, 512], replicated, may hold values from -0.25 to 0.25
- queries: bfloat16 [128, 512], replicated, may hold values from -64 to 64
Outputs:
- prediction_matrix: bfloat16 [4, 128, 512], P(('groups', 'series'), 'tm'), parts along dimension 0
The draws below stay inside these ranges and needn't reach their ends.
There are 2 independent parts, one for each index of `groups`. The reference program is written for one: setup_inputs(seed, part) draws one part's arguments, and reference() takes and returns one part's arrays. A program takes and returns all parts, laid end to end along the dimension named above; an argument that names none is the same for every part. Nothing has to cross between parts.
All inputs are finite; a program needn't handle non-finite values.
Results may differ from the reference program's by a relative error of at most 0.033.
Values may be sent and summed in bfloat16 or wider, within the bound.
No kernel may reach another device: no remote copies, remote signals or barrier semaphores. Data moves between devices by JAX's collectives and lax.ppermute only.
A program may use at most 128 MiB of HBM per device.

```python
import jax
import jax.numpy as jnp
from jax import lax

D = 512
FF = 1024
HEADS = 8
HEAD_DIM = 64
HORIZON = 128
FIRST_DILATION = 256
SECOND_DILATION = 512
LENGTH = 8192
SERIES = 2


def draw_queries(key, part):
    key = jax.random.fold_in(key, 7)
    key_base = jax.random.fold_in(key, 1)
    base = jnp.clip(jax.random.normal(key_base, (HORIZON, D), jnp.float32), -4.0, 4.0) * 3.0
    return base.astype(jnp.bfloat16)


def block_scale(key, dims, pieces, least, top_value):
    loudness, own = 1.0, jax.random.fold_in(key, 6)
    for position, blocks in pieces:
        heights = jnp.exp(jax.random.uniform(jax.random.fold_in(own, position), (blocks,), jnp.float32, least / len(pieces), top_value / len(pieces)))
        loudness = loudness * jnp.repeat(heights, dims[position] // blocks).reshape([-1 if axis == position else 1 for axis in range(len(dims))])
    return loudness


def centred(key, extent, spread, most, cuts=(), dtype=jnp.bfloat16):
    entries = spread * jax.random.normal(key, extent, jnp.float32)
    if cuts:
        entries = entries * block_scale(key, extent, cuts, -0.22, 0.18)
    return jnp.clip(entries, -most, most).astype(dtype)


def setup_inputs(seed: int = 0, part: int = 0) -> dict:
    streams_of = jax.random.split(jax.random.key(seed), 9)
    own_keys = jax.random.split(jax.random.fold_in(streams_of[8], part), 9)
    return {
        "history": centred(own_keys[0], (SERIES, LENGTH, D), 1.0, 6.0, ((0, 2), (1, 8))),
        "convolution_taps": centred(streams_of[1], (2, 3, D), 0.7, 3.0, (), jnp.float32),
        "norm_gain_pair": jnp.clip(1.0 + 0.15 * jax.random.normal(streams_of[2], (2, D), jnp.float32), 0.25, 1.75),
        "up_projection": centred(streams_of[3], (2, D, FF), D ** -0.5, 0.25),
        "down_projection": centred(streams_of[4], (2, FF, D), FF ** -0.5, 0.1875),
        "w_kv": centred(streams_of[5], (D, 2 * D), D ** -0.5, 0.25),
        "readout_matrix": centred(streams_of[6], (D, D), D ** -0.5, 0.25),
        "queries": draw_queries(jax.random.fold_in(streams_of[8], 71), part),
    }


def channel_mixer(sequence_input, taps, gain, up_weight, down_weight, dilation):
    values = sequence_input.astype(jnp.float32)
    length = values.shape[0]
    mixed = taps[0] * values
    for step in (1, 2):
        offset = step * dilation
        shifted_values = jnp.concatenate([jnp.zeros((offset, values.shape[1]), jnp.float32), values[:length - offset]], axis=0)
        mixed = mixed + taps[step] * shifted_values
    scaled = mixed * lax.rsqrt(lax.optimization_barrier(jnp.mean(mixed * mixed, axis=-1, keepdims=True)) + 1e-05) * gain
    normed = scaled.astype(jnp.bfloat16)
    inner = jax.nn.gelu(jnp.dot(normed, up_weight, preferred_element_type=jnp.float32), approximate=True).astype(jnp.bfloat16)
    return (values + jnp.dot(inner, down_weight, preferred_element_type=jnp.float32)).astype(jnp.bfloat16)

def attend(sequence_input, w_kv, queries):
    length = sequence_input.shape[0]
    pairs = jnp.dot(sequence_input, w_kv, preferred_element_type=jnp.float32).astype(jnp.bfloat16)
    keys = pairs[:, :D].reshape(length, HEADS, HEAD_DIM).transpose(1, 0, 2)
    values = pairs[:, D:].reshape(length, HEADS, HEAD_DIM).transpose(1, 0, 2)
    asked = queries.reshape(HORIZON, HEADS, HEAD_DIM).transpose(1, 0, 2)

    def one_head(items):
        query, key, value = items
        scores = jnp.dot(query, key.T, preferred_element_type=jnp.float32) * HEAD_DIM ** (-0.5)
        top = lax.optimization_barrier(jnp.max(scores, axis=-1, keepdims=True))
        expo = jnp.exp(scores - top)
        total = lax.optimization_barrier(jnp.sum(expo, axis=-1, keepdims=True))
        weights = expo.astype(jnp.bfloat16)
        return jnp.dot(weights, value, preferred_element_type=jnp.float32) / total
    context = lax.map(one_head, (asked, keys, values))
    return context.transpose(1, 0, 2).reshape(HORIZON, D).astype(jnp.bfloat16)

def reference(history, convolution_taps, norm_gain_pair, up_projection, down_projection, w_kv, readout_matrix, queries):
    results = []
    for member in range(SERIES):
        sequence_input = history[member]
        sequence_input = channel_mixer(sequence_input, convolution_taps[0], norm_gain_pair[0], up_projection[0], down_projection[0], FIRST_DILATION)
        sequence_input = channel_mixer(sequence_input, convolution_taps[1], norm_gain_pair[1], up_projection[1], down_projection[1], SECOND_DILATION)
        context = attend(sequence_input, w_kv, queries)
        results.append(jnp.dot(context, readout_matrix, preferred_element_type=jnp.float32).astype(jnp.bfloat16))
    return jnp.stack(results)
```

```python
import functools

import jax
import jax.numpy as jnp
from jax import lax
from jax.experimental import pallas as pl
from jax.experimental.pallas import tpu as pltpu
from jax.sharding import PartitionSpec as P

HEADS = 8
STEP = 256
HALF = STEP // 2
BF16, F32 = jnp.bfloat16, jnp.float32
ANY = pl.BlockSpec(memory_space=pl.ANY)
VMEM = pl.BlockSpec(memory_space=pltpu.VMEM)


def dot(a, b):
    return jnp.dot(a, b, preferred_element_type=F32)


def gelu(u):
    return 0.5 * u * (1.0 + jnp.tanh(0.7978845608028654 * (u + 0.044715 * (u * u * u))))


def mix(src, first, steps, dilation, taps, gain, up, down, factors):
    rows, kept = [], []
    for j in range(steps):
        w1, w2 = factors[j]
        at = [(first + j - k * dilation) * HALF for k in range(3)]
        now = src[at[0] : at[0] + HALF, :].astype(F32)
        conv = taps[0:1, :] * now
        conv = conv + (taps[1:2, :] * w1) * src[at[1] : at[1] + HALF, :].astype(F32)
        conv = conv + (taps[2:3, :] * w2) * src[at[2] : at[2] + HALF, :].astype(F32)
        scale = lax.rsqrt(jnp.mean(conv * conv, axis=-1, keepdims=True) + 1e-05)
        rows.append((conv * scale * gain).astype(BF16))
        kept.append(now)
    inner = gelu(dot(jnp.concatenate(rows, 0), up)).astype(BF16)
    return (jnp.concatenate(kept, 0) + dot(inner, down)).astype(BF16)


def attend(x2, w_kv, queries):
    pairs = dot(x2, w_kv).astype(BF16)
    horizon, width = queries.shape
    low = lax.broadcasted_iota(jnp.int32, (horizon, 128), 1) < 64
    zero = jnp.zeros((horizon, 128), BF16)
    acc, top, total = [], [], []
    for p in range(width // 128):
        lanes = slice(128 * p, 128 * p + 128)
        q = queries[:, lanes] * jnp.asarray(0.125, BF16)
        q2 = jnp.concatenate([jnp.where(low, q, zero), jnp.where(low, zero, q)], 0)
        scores = lax.dot_general(q2, pairs[:, lanes], (((1,), (1,)), ((), ())), preferred_element_type=F32)
        m = jnp.max(scores, axis=-1, keepdims=True)
        e = jnp.exp(scores - m)
        s = jnp.sum(e, axis=-1, keepdims=True)
        c = dot(e.astype(BF16), pairs[:, width + 128 * p : width + 128 * p + 128])
        acc.append(jnp.where(low, c[:horizon], c[horizon:]))
        top.append(jnp.where(low, m[:horizon], m[horizon:]))
        total.append(jnp.where(low, s[:horizon], s[horizon:]))
    return jnp.concatenate(acc, 1), jnp.concatenate(top, 1), jnp.concatenate(total, 1)


def encode(context, lse):
    width = lse.shape[1]
    row = lax.broadcasted_iota(jnp.int32, (width, 128), 0)
    col = lax.broadcasted_iota(jnp.int32, (width, 128), 1)
    stats, rest = jnp.zeros((lse.shape[0], 128), F32), lse
    for piece in range(3):
        part = rest.astype(BF16)
        pick = (row == 64 * (col - 8 * piece)) & (col >= 8 * piece) & (col < 8 * piece + 8)
        stats = stats + dot(part, pick.astype(BF16))
        rest = rest - part.astype(F32)
    return jnp.concatenate([context.astype(BF16), stats.astype(BF16)], 1)


def decode(rows):
    width = rows.shape[1] - 128
    row = lax.broadcasted_iota(jnp.int32, (128, width), 0)
    col = lax.broadcasted_iota(jnp.int32, (128, width), 1)
    spread = ((row % 8 == col // 64) & (row < 24)).astype(BF16)
    return rows[:, :width].astype(F32), dot(rows[:, width:], spread)


def combine(parts):
    top = functools.reduce(jnp.maximum, [l for _, l in parts])
    weights = [jnp.exp(l - top) for _, l in parts]
    total = functools.reduce(jnp.add, weights)
    context = functools.reduce(jnp.add, [w * c for w, (c, _) in zip(weights, parts)])
    return context / total, top + jnp.log(total)


def valid(side):
    here, count = lax.axis_index("tm"), lax.axis_size("tm")
    return jnp.where(here == count - 2 + side, 0.0, 1.0).astype(F32)


def early_kernel(hist, got, near, taps, gains, up, down, w_kv, queries, tail, acc, top, total,
                 x0, x1, up_v, down_v, kv_v, sem):
    side = lax.rem(lax.axis_index("tm"), 2)
    mine = pl.ds(pl.multiple_of(side * HALF, HALF), HALF)
    own_at = side * 7
    copies = [
        pltpu.make_async_copy(up, up_v, sem.at[0]),
        pltpu.make_async_copy(down, down_v, sem.at[1]),
        pltpu.make_async_copy(w_kv, kv_v, sem.at[2]),
        pltpu.make_async_copy(hist.at[:, mine, :], x0.at[pl.ds(own_at, 4)], sem.at[3]),
        pltpu.make_async_copy(got, x0.at[pl.ds(4 - side, 4)], sem.at[4]),
        pltpu.make_async_copy(near, x0.at[pl.ds(8 - 8 * side, 3)], sem.at[5]),
    ]
    for i in (3, 4, 5, 0, 1, 2):
        copies[i].start()
    v = valid(0)
    one = 1.0
    for i in (3, 4, 5):
        copies[i].wait()
    rows0 = x0.reshape(11 * HALF, x0.shape[-1])
    copies[0].wait()
    copies[1].wait()
    for j in range(0, 9, 3):
        factors = [(v, v), (one, v), (one, one)] if j == 6 else [(one, one)] * 3
        x1[j * HALF : (j + 3) * HALF, :] = mix(
            rows0, j + 2, 3, 1, taps[0], gains[0:1, :], up_v[0], down_v[0], factors
        )
    tail[...] = x1[pl.ds(pl.multiple_of(side * (5 * HALF), HALF), 4 * HALF), :]
    x2 = jnp.concatenate([
        mix(x1, 4, 2, 2, taps[1], gains[1:2, :], up_v[1], down_v[1], [(one, one)] * 2),
        mix(x1, 6, 3, 2, taps[1], gains[1:2, :], up_v[1], down_v[1], [(v, v), (v, v), (one, v)]),
    ], 0)
    copies[2].wait()
    acc[...], top[...], total[...] = attend(x2, kv_v[...], queries[...])


def late_kernel(hist, far, tail, acc, top, total, taps, gains, up, down, w_kv, queries, out,
                x0, x1, up_v, down_v, kv_v, sem):
    side = lax.rem(lax.axis_index("tm"), 2)
    mine = pl.ds(pl.multiple_of(side * HALF, HALF), HALF)
    copies = [
        pltpu.make_async_copy(up, up_v, sem.at[0]),
        pltpu.make_async_copy(down, down_v, sem.at[1]),
        pltpu.make_async_copy(w_kv, kv_v, sem.at[2]),
        pltpu.make_async_copy(hist.at[pl.ds(2 * side, 2), mine, :], x0.at[pl.ds(3 - 3 * side, 2)], sem.at[3]),
        pltpu.make_async_copy(far, x0.at[pl.ds(2 * side, 3)], sem.at[4]),
    ]
    for i in (3, 4, 0, 1, 2):
        copies[i].start()
    x1[pl.ds(pl.multiple_of((3 - 3 * side) * HALF, HALF), 4 * HALF), :] = tail[...]
    v = valid(1)
    one = 1.0
    copies[3].wait()
    copies[4].wait()
    rows0 = x0.reshape(5 * HALF, x0.shape[-1])
    copies[0].wait()
    copies[1].wait()
    fresh = mix(rows0, 2, 3, 1, taps[0], gains[0:1, :], up_v[0], down_v[0], [(v, v), (one, v), (one, one)])
    x1[pl.ds(pl.multiple_of(side * (4 * HALF), HALF), 3 * HALF), :] = fresh
    x2 = mix(x1, 4, 3, 2, taps[1], gains[1:2, :], up_v[1], down_v[1], [(v, v), (v, v), (one, v)])
    copies[2].wait()
    acc2, top2, total2 = attend(x2, kv_v[...], queries[...])
    best = jnp.maximum(top[...], top2)
    a, b = jnp.exp(top[...] - best), jnp.exp(top2 - best)
    whole = total[...] * a + total2 * b
    out[...] = encode((acc[...] * a + acc2 * b) / whole, best + jnp.log(whole))


def pair_kernel(mine, theirs, out):
    shape = mine.shape
    flat = (shape[0] * shape[1], shape[2])
    context, lse = combine([decode(mine[...].reshape(flat)), decode(theirs[...].reshape(flat))])
    out[...] = encode(context, lse).reshape(shape)


def final_kernel(count, *refs):
    parts, readout, out = refs[:count], refs[count], refs[count + 1]
    context, _ = combine([decode(part[...]) for part in parts])
    out[...] = dot(context.astype(BF16), readout[...]).astype(BF16)


def on_device(history, taps, gains, up, down, w_kv, readout, queries):
    _, span, width = history.shape
    horizon, hidden = queries.shape[0], up.shape[-1]
    count = lax.axis_size("tm")
    here = lax.axis_index("tm")
    side, pair = lax.rem(here, 2), lax.div(here, 2)
    n_pairs = count // 2
    share = horizon // count

    hist = history.reshape(span // STEP, STEP, width)
    other = (1 - side) * HALF
    swap = [(i, i ^ 1) for i in range(count)]
    ahead = [(2 * p + 1, 2 * p + 2) for p in range(n_pairs - 1)]
    behind = [(2 * p, (2 * p - 2) % count) for p in range(n_pairs)]
    near_pairs = [(s, t + 1) for s, t in ahead] + behind
    far_pairs = ahead + [(s, t + 1) for s, t in behind]
    zero = jnp.zeros_like(side)
    out_swap = lax.dynamic_slice(hist, (zero, other, zero), (4, HALF, width))
    got = lax.ppermute(out_swap, "tm", swap)
    near = lax.ppermute(
        lax.dynamic_slice(hist, (side, side * HALF, zero), (3, HALF, width)), "tm", near_pairs
    )
    far_out = lax.dynamic_slice(hist, (side, other, zero), (3, HALF, width))
    far_out, got = lax.optimization_barrier((far_out, got))
    far = lax.ppermute(far_out, "tm", far_pairs)

    state = jax.ShapeDtypeStruct((horizon, width), F32)
    weights = [
        pltpu.VMEM(up.shape, BF16), pltpu.VMEM(down.shape, BF16), pltpu.VMEM(w_kv.shape, BF16),
        pltpu.SemaphoreType.DMA((6,)),
    ]
    per_row = 4 * width * hidden
    tail, acc, top, total = pl.pallas_call(
        early_kernel,
        out_shape=[jax.ShapeDtypeStruct((4 * HALF, width), BF16), state, state, state],
        in_specs=[ANY] * 3 + [VMEM] * 2 + [ANY] * 3 + [VMEM],
        out_specs=[VMEM] * 4,
        scratch_shapes=[pltpu.VMEM((11, HALF, width), BF16), pltpu.VMEM((9 * HALF, width), BF16)] + weights,
        compiler_params=pltpu.CompilerParams(vmem_limit_bytes=40 * 1024 * 1024),
        cost_estimate=pl.CostEstimate(
            flops=(14 * per_row + 5 * 2 * per_row) * HALF, bytes_accessed=8 << 20, transcendentals=2 << 20
        ),
        name="early",
    )(hist, got, near, taps, gains, up, down, w_kv, queries)
    payload = pl.pallas_call(
        late_kernel,
        out_shape=jax.ShapeDtypeStruct((horizon, width + 128), BF16),
        in_specs=[ANY] * 2 + [VMEM] * 6 + [ANY] * 3 + [VMEM],
        out_specs=VMEM,
        scratch_shapes=[pltpu.VMEM((5, HALF, width), BF16), pltpu.VMEM((7 * HALF, width), BF16)] + weights,
        compiler_params=pltpu.CompilerParams(vmem_limit_bytes=40 * 1024 * 1024),
        cost_estimate=pl.CostEstimate(
            flops=(6 * per_row + 3 * 2 * per_row) * HALF, bytes_accessed=8 << 20, transcendentals=1 << 20
        ),
        name="late",
    )(hist, far, tail, acc, top, total, taps, gains, up, down, w_kv, queries)

    lanes = payload.shape[-1]
    split = payload.reshape(n_pairs, 2, share, lanes)
    theirs = lax.ppermute(lax.dynamic_index_in_dim(split, 1 - side, 1, False), "tm", swap)
    merged = pl.pallas_call(
        pair_kernel,
        out_shape=jax.ShapeDtypeStruct((n_pairs, share, lanes), BF16),
        in_specs=[VMEM] * 2,
        out_specs=VMEM,
        name="pair",
    )(lax.dynamic_index_in_dim(split, side, 1, False), theirs)
    if n_pairs <= 4 and n_pairs & (n_pairs - 1) == 0:
        parts = [lax.dynamic_index_in_dim(merged, pair, 0, False)]
        for s in range(1, n_pairs):
            block = lax.dynamic_index_in_dim(merged, pair ^ s, 0, False)
            parts.append(lax.ppermute(block, "tm", [(i, i ^ (2 * s)) for i in range(count)]))
    else:
        groups = [[2 * p + s for p in range(n_pairs)] for s in range(2)]
        swapped = lax.all_to_all(merged, "tm", 0, 0, axis_index_groups=groups, tiled=True)
        parts = [swapped[p] for p in range(n_pairs)]
    result = pl.pallas_call(
        functools.partial(final_kernel, len(parts)),
        out_shape=jax.ShapeDtypeStruct((share, width), BF16),
        in_specs=[VMEM] * (len(parts) + 1),
        out_specs=VMEM,
        name="final",
    )(*parts, readout)
    return result[None]


def solution(mesh):
    placed = (P(("groups", "series"), "tm", None), P(), P(), P(), P(), P(), P(), P())
    return jax.shard_map(
        on_device,
        mesh=mesh,
        in_specs=placed,
        out_specs=P(("groups", "series"), "tm", None),
        check_vma=False,
    )
```

```python
import functools

import jax
import jax.numpy as jnp
from jax import lax
from jax.experimental import pallas as pl
from jax.experimental.pallas import tpu as pltpu
from jax.sharding import PartitionSpec as P

HEADS = 8
STEP = 256
HALF = STEP // 2
BF16, F32 = jnp.bfloat16, jnp.float32
ANY = pl.BlockSpec(memory_space=pl.ANY)
VMEM = pl.BlockSpec(memory_space=pltpu.VMEM)
HBM = pl.BlockSpec(memory_space=pltpu.HBM)


def dot(a, b):
    return jnp.dot(a, b, preferred_element_type=F32)


def gelu(u):
    return 0.5 * u * (1.0 + jnp.tanh(0.7978845608028654 * (u + 0.044715 * (u * u * u))))


def mix(src, first, steps, dilation, taps, gain, up, down, factors):
    rows, kept = [], []
    for j in range(steps):
        w1, w2 = factors[j]
        at = [(first + j - k * dilation) * HALF for k in range(3)]
        now = src[at[0] : at[0] + HALF, :].astype(F32)
        conv = taps[0:1, :] * now
        conv = conv + (taps[1:2, :] * w1) * src[at[1] : at[1] + HALF, :].astype(F32)
        conv = conv + (taps[2:3, :] * w2) * src[at[2] : at[2] + HALF, :].astype(F32)
        scale = lax.rsqrt(jnp.mean(conv * conv, axis=-1, keepdims=True) + 1e-05)
        rows.append((conv * scale * gain).astype(BF16))
        kept.append(now)
    inner = gelu(dot(jnp.concatenate(rows, 0), up)).astype(BF16)
    return (jnp.concatenate(kept, 0) + dot(inner, down)).astype(BF16)


def attend(x2, w_kv, queries):
    pairs = dot(x2, w_kv).astype(BF16)
    horizon, width = queries.shape
    low = lax.broadcasted_iota(jnp.int32, (horizon, 128), 1) < 64
    zero = jnp.zeros((horizon, 128), BF16)
    acc, top, total = [], [], []
    for p in range(width // 128):
        lanes = slice(128 * p, 128 * p + 128)
        q = queries[:, lanes] * jnp.asarray(0.125, BF16)
        q2 = jnp.concatenate([jnp.where(low, q, zero), jnp.where(low, zero, q)], 0)
        scores = lax.dot_general(q2, pairs[:, lanes], (((1,), (1,)), ((), ())), preferred_element_type=F32)
        m = jnp.max(scores, axis=-1, keepdims=True)
        e = jnp.exp(scores - m)
        s = jnp.sum(e, axis=-1, keepdims=True)
        c = dot(e.astype(BF16), pairs[:, width + 128 * p : width + 128 * p + 128])
        acc.append(jnp.where(low, c[:horizon], c[horizon:]))
        top.append(jnp.where(low, m[:horizon], m[horizon:]))
        total.append(jnp.where(low, s[:horizon], s[horizon:]))
    return jnp.concatenate(acc, 1), jnp.concatenate(top, 1), jnp.concatenate(total, 1)


def encode(context, lse):
    lane = lax.broadcasted_iota(jnp.int32, (lse.shape[0], 128), 1) & 63
    stats = jnp.zeros((lse.shape[0], 128), F32)
    for p in range(lse.shape[1] // 128):
        rest = lse[:, 128 * p : 128 * p + 128]
        for piece in range(3):
            part = rest.astype(BF16).astype(F32)
            stats = jnp.where(lane == 3 * p + piece, part, stats)
            rest = rest - part
    return jnp.concatenate([context.astype(BF16), stats.astype(BF16)], 1)


def spread_matrix(width):
    row = lax.broadcasted_iota(jnp.int32, (128, width), 0)
    col = lax.broadcasted_iota(jnp.int32, (128, width), 1)
    piece = (row & 63) - 3 * (col >> 7)
    return jnp.where((piece >= 0) & (piece < 3) & ((row >> 6) == ((col >> 6) & 1)), 1.0, 0.0).astype(BF16)


def decode(rows, spread):
    width = rows.shape[1] - 128
    return rows[:, :width].astype(F32), dot(rows[:, width:], spread)


def combine(parts):
    top = functools.reduce(jnp.maximum, [l for _, l in parts])
    weights = [jnp.exp(l - top) for _, l in parts]
    total = functools.reduce(jnp.add, weights)
    context = functools.reduce(jnp.add, [w * c for w, (c, _) in zip(weights, parts)])
    return context / total, top + jnp.log(total)


def valid(side):
    here, count = lax.axis_index("tm"), lax.axis_size("tm")
    return jnp.where(here == count - 2 + side, 0.0, 1.0).astype(F32)


def early_kernel(own, got, near, taps, gains, up_v, down_v, kv_v, queries, tail, acc, top, total,
                 x0, x1, sem):
    side = lax.rem(lax.axis_index("tm"), 2)
    copies = [
        pltpu.make_async_copy(own, x0.at[pl.ds(side * 7, 4)], sem.at[0]),
        pltpu.make_async_copy(got, x0.at[pl.ds(4 - side, 4)], sem.at[1]),
        pltpu.make_async_copy(near, x0.at[pl.ds(8 - 8 * side, 3)], sem.at[2]),
    ]
    for copy in copies:
        copy.start()
    v = valid(0)
    one = 1.0
    for copy in copies:
        copy.wait()
    rows0 = x0.reshape(11 * HALF, x0.shape[-1])
    for j in range(0, 9, 3):
        factors = [(v, v), (one, v), (one, one)] if j == 6 else [(one, one)] * 3
        x1[j * HALF : (j + 3) * HALF, :] = mix(
            rows0, j + 2, 3, 1, taps[0], gains[0:1, :], up_v[0], down_v[0], factors
        )
    tail[...] = x1[pl.ds(pl.multiple_of(side * (5 * HALF), HALF), 4 * HALF), :]
    x2 = jnp.concatenate([
        mix(x1, 4, 2, 2, taps[1], gains[1:2, :], up_v[1], down_v[1], [(one, one)] * 2),
        mix(x1, 6, 3, 2, taps[1], gains[1:2, :], up_v[1], down_v[1], [(v, v), (v, v), (one, v)]),
    ], 0)
    acc[...], top[...], total[...] = attend(x2, kv_v[...], queries[...])


def late_kernel(own, far, tail, acc, top, total, taps, gains, up_v, down_v, kv_v, queries, *refs):
    outs, (x0, x1, sem) = refs[:-3], refs[-3:]
    side = lax.rem(lax.axis_index("tm"), 2)
    copies = [
        pltpu.make_async_copy(own.at[pl.ds(2 * side, 2)], x0.at[pl.ds(3 - 3 * side, 2)], sem.at[0]),
        pltpu.make_async_copy(far, x0.at[pl.ds(2 * side, 3)], sem.at[1]),
    ]
    for copy in copies:
        copy.start()
    x1[pl.ds(pl.multiple_of((3 - 3 * side) * HALF, HALF), 4 * HALF), :] = tail[...]
    v = valid(1)
    one = 1.0
    for copy in copies:
        copy.wait()
    rows0 = x0.reshape(5 * HALF, x0.shape[-1])
    fresh = mix(rows0, 2, 3, 1, taps[0], gains[0:1, :], up_v[0], down_v[0], [(v, v), (one, v), (one, one)])
    x1[pl.ds(pl.multiple_of(side * (4 * HALF), HALF), 3 * HALF), :] = fresh
    x2 = mix(x1, 4, 3, 2, taps[1], gains[1:2, :], up_v[1], down_v[1], [(v, v), (v, v), (one, v)])
    acc2, top2, total2 = attend(x2, kv_v[...], queries[...])
    best = jnp.maximum(top[...], top2)
    a, b = jnp.exp(top[...] - best), jnp.exp(top2 - best)
    whole = total[...] * a + total2 * b
    rows = encode((acc[...] * a + acc2 * b) / whole, best + jnp.log(whole))
    if len(outs) == 1:
        outs[0][...] = rows
        return
    n_pairs, share, lanes = outs[0].shape
    split = rows.reshape(n_pairs, 2, share, lanes)
    outs[0][...] = jnp.where(side == 0, split[:, 0], split[:, 1])
    outs[1][...] = jnp.where(side == 0, split[:, 1], split[:, 0])


def pack_kernel(n, hist, *refs):
    side = lax.rem(lax.axis_index("tm"), 2)
    mine = pl.ds(pl.multiple_of(side * HALF, HALF), HALF)
    other = pl.ds(pl.multiple_of((1 - side) * HALF, HALF), HALF)
    three = pl.ds(side, 3)
    if n == 0:
        swap_out, sem = refs
        copies = [pltpu.make_async_copy(hist.at[:, other, :], swap_out, sem.at[0])]
    elif n == 2:
        whole, (own_out, *outs, sem) = refs[:4], refs[4:]
        copies = [
            pltpu.make_async_copy(a, b, sem.at[i]) for i, (a, b) in enumerate(zip(whole, outs))
        ] + [pltpu.make_async_copy(hist.at[:, mine, :], own_out, sem.at[4])]
    else:
        near_out, far_out, sem = refs
        copies = [
            pltpu.make_async_copy(hist.at[three, mine, :], near_out, sem.at[0]),
            pltpu.make_async_copy(hist.at[three, other, :], far_out, sem.at[1]),
        ]
    for copy in copies:
        copy.start()
    for copy in copies:
        copy.wait()


def pair_kernel(mine, theirs, *refs):
    shape = mine.shape
    flat = (shape[0] * shape[1], shape[2])
    spread = spread_matrix(shape[2] - 128)
    context, lse = combine([
        decode(mine[...].reshape(flat), spread), decode(theirs[...].reshape(flat), spread)
    ])
    merged = encode(context, lse).reshape(shape)
    if len(refs) == 1:
        refs[0][...] = merged
        return
    held = refs[-1]
    held[...] = merged
    pair = lax.div(lax.axis_index("tm"), 2)
    for s, out in enumerate(refs[:-1]):
        out[...] = held[pair ^ s]


def final_kernel(count, *refs):
    parts, readout, out = refs[:count], refs[count], refs[count + 1]
    spread = spread_matrix(out.shape[1])
    context, _ = combine([decode(part[...], spread) for part in parts])
    out[...] = dot(context.astype(BF16), readout[...]).astype(BF16)


def small(limit=8):
    return pltpu.CompilerParams(vmem_limit_bytes=limit * 1024 * 1024)


def on_device(history, taps, gains, up, down, w_kv, readout, queries):
    _, span, width = history.shape
    horizon, hidden = queries.shape[0], up.shape[-1]
    count = lax.axis_size("tm")
    here = lax.axis_index("tm")
    side, pair = lax.rem(here, 2), lax.div(here, 2)
    n_pairs = count // 2
    share = horizon // count

    hist = history.reshape(span // STEP, STEP, width)
    swap = [(i, i ^ 1) for i in range(count)]
    ahead = [(2 * p + 1, 2 * p + 2) for p in range(n_pairs - 1)]
    behind = [(2 * p, (2 * p - 2) % count) for p in range(n_pairs)]
    near_pairs = [(s, t + 1) for s, t in ahead] + behind
    far_pairs = ahead + [(s, t + 1) for s, t in behind]
    three = jax.ShapeDtypeStruct((3, HALF, width), BF16)
    swap_out = pl.pallas_call(
        functools.partial(pack_kernel, 0),
        out_shape=jax.ShapeDtypeStruct((4, HALF, width), BF16),
        in_specs=[HBM],
        out_specs=VMEM,
        scratch_shapes=[pltpu.SemaphoreType.DMA((1,))],
        compiler_params=small(),
        name="pack_swap",
    )(hist)
    got = lax.ppermute(swap_out, "tm", swap)
    near_out, far_out = pl.pallas_call(
        functools.partial(pack_kernel, 1),
        out_shape=[three, three],
        in_specs=[HBM],
        out_specs=[VMEM, VMEM],
        scratch_shapes=[pltpu.SemaphoreType.DMA((2,))],
        compiler_params=small(),
        name="pack_halo",
    )(hist)
    near = lax.ppermute(near_out, "tm", near_pairs)
    far = lax.ppermute(far_out, "tm", far_pairs)

    own, up_v, down_v, kv_v, readout_v = pl.pallas_call(
        functools.partial(pack_kernel, 2),
        out_shape=[jax.ShapeDtypeStruct((4, HALF, width), BF16)]
        + [jax.ShapeDtypeStruct(w.shape, w.dtype) for w in (up, down, w_kv, readout)],
        in_specs=[HBM] * 5,
        out_specs=[VMEM] * 5,
        scratch_shapes=[pltpu.SemaphoreType.DMA((5,))],
        compiler_params=small(16),
        name="stage",
    )(hist, up, down, w_kv, readout)
    state = jax.ShapeDtypeStruct((horizon, width), F32)
    per_row = 4 * width * hidden
    tail, acc, top, total = pl.pallas_call(
        early_kernel,
        out_shape=[jax.ShapeDtypeStruct((4 * HALF, width), BF16), state, state, state],
        in_specs=[ANY] * 3 + [VMEM] * 6,
        out_specs=[VMEM] * 4,
        scratch_shapes=[
            pltpu.VMEM((11, HALF, width), BF16), pltpu.VMEM((9 * HALF, width), BF16), pltpu.SemaphoreType.DMA((3,))
        ],
        compiler_params=pltpu.CompilerParams(vmem_limit_bytes=32 * 1024 * 1024),
        cost_estimate=pl.CostEstimate(
            flops=(14 * per_row + 5 * 2 * per_row) * HALF, bytes_accessed=8 << 20, transcendentals=2 << 20
        ),
        name="early",
    )(own, got, near, taps, gains, up_v, down_v, kv_v, queries)
    lanes = width + 128
    fused = share % 16 == 0 and n_pairs <= 4 and n_pairs & (n_pairs - 1) == 0
    one = jax.ShapeDtypeStruct((share, lanes), BF16)
    quarter = jax.ShapeDtypeStruct((n_pairs, share, lanes), BF16)
    payload = pl.pallas_call(
        late_kernel,
        out_shape=[quarter, quarter] if fused else [jax.ShapeDtypeStruct((horizon, lanes), BF16)],
        in_specs=[ANY] * 2 + [VMEM] * 10,
        out_specs=[VMEM] * (2 if fused else 1),
        scratch_shapes=[
            pltpu.VMEM((5, HALF, width), BF16), pltpu.VMEM((7 * HALF, width), BF16), pltpu.SemaphoreType.DMA((2,))
        ],
        compiler_params=pltpu.CompilerParams(vmem_limit_bytes=32 * 1024 * 1024),
        cost_estimate=pl.CostEstimate(
            flops=(6 * per_row + 3 * 2 * per_row) * HALF, bytes_accessed=8 << 20, transcendentals=1 << 20
        ),
        name="late",
    )(own, far, tail, acc, top, total, taps, gains, up_v, down_v, kv_v, queries)
    if fused:
        mine, send = payload
    else:
        split = payload[0].reshape(n_pairs, 2, share, lanes)
        mine, send = (lax.dynamic_index_in_dim(split, s, 1, False) for s in (side, 1 - side))
    theirs = lax.ppermute(send, "tm", swap)
    merged = pl.pallas_call(
        pair_kernel,
        out_shape=[one] * n_pairs if fused else [quarter],
        in_specs=[VMEM] * 2,
        out_specs=[VMEM] * (n_pairs if fused else 1),
        scratch_shapes=[pltpu.VMEM(quarter.shape, BF16)] if fused else [],
        compiler_params=small(),
        name="pair",
    )(mine, theirs)
    if fused:
        parts = [merged[0]] + [
            lax.ppermute(merged[s], "tm", [(i, i ^ (2 * s)) for i in range(count)]) for s in range(1, n_pairs)
        ]
    else:
        groups = [[2 * p + s for p in range(n_pairs)] for s in range(2)]
        swapped = lax.all_to_all(merged[0], "tm", 0, 0, axis_index_groups=groups, tiled=True)
        parts = [swapped[p] for p in range(n_pairs)]
    result = pl.pallas_call(
        functools.partial(final_kernel, len(parts)),
        out_shape=jax.ShapeDtypeStruct((share, width), BF16),
        in_specs=[VMEM] * (len(parts) + 1),
        out_specs=VMEM,
        compiler_params=small(),
        name="final",
    )(*parts, readout_v)
    return result[None]


def solution(mesh):
    placed = (P(("groups", "series"), "tm", None), P(), P(), P(), P(), P(), P(), P())
    return jax.shard_map(
        on_device,
        mesh=mesh,
        in_specs=placed,
        out_specs=P(("groups", "series"), "tm", None),
        check_vma=False,
    )
```

```python
import functools

import jax
import jax.numpy as jnp
from jax import lax
from jax.experimental import pallas as pl
from jax.experimental.pallas import tpu as pltpu
from jax.sharding import PartitionSpec as P

HEADS = 8
STEP = 256
HALF = STEP // 2
BF16, F32 = jnp.bfloat16, jnp.float32
ANY = pl.BlockSpec(memory_space=pl.ANY)
VMEM = pl.BlockSpec(memory_space=pltpu.VMEM)
HBM = pl.BlockSpec(memory_space=pltpu.HBM)


def dot(a, b):
    return jnp.dot(a, b, preferred_element_type=F32)


def gelu(u):
    half = 0.5 * u
    return half + half * jnp.tanh(u * (0.7978845608028654 + (0.7978845608028654 * 0.044715) * (u * u)))


def mix(src, first, steps, dilation, taps, gain, up, down, factors):
    rows, kept = [], []
    for j in range(steps):
        w1, w2 = factors[j]
        at = [(first + j - k * dilation) * HALF for k in range(3)]
        now = src[at[0] : at[0] + HALF, :].astype(F32)
        conv = taps[0:1, :] * now
        conv = conv + (taps[1:2, :] * w1) * src[at[1] : at[1] + HALF, :].astype(F32)
        conv = conv + (taps[2:3, :] * w2) * src[at[2] : at[2] + HALF, :].astype(F32)
        scale = lax.rsqrt(jnp.mean(conv * conv, axis=-1, keepdims=True) + 1e-05)
        rows.append((conv * scale * gain).astype(BF16))
        kept.append(now)
    inner = gelu(dot(jnp.concatenate(rows, 0), up)).astype(BF16)
    return (jnp.concatenate(kept, 0) + dot(inner, down)).astype(BF16)


def attend(x2, w_kv, queries):
    pairs = dot(x2, w_kv).astype(BF16)
    horizon, width = queries.shape
    low = lax.broadcasted_iota(jnp.int32, (horizon, 128), 1) < 64
    zero = jnp.zeros((horizon, 128), BF16)
    acc, top, total, scores = [], [], [], []
    for p in range(width // 128):
        lanes = slice(128 * p, 128 * p + 128)
        q = queries[:, lanes] * jnp.asarray(0.125, BF16)
        q2 = jnp.concatenate([jnp.where(low, q, zero), jnp.where(low, zero, q)], 0)
        scores.append(
            lax.dot_general(q2, pairs[:, lanes], (((1,), (1,)), ((), ())), preferred_element_type=F32)
        )
    for p in range(width // 128):
        m = jnp.max(scores[p], axis=-1, keepdims=True)
        e = jnp.exp(scores[p] - m)
        s = jnp.sum(e, axis=-1, keepdims=True)
        c = dot(e.astype(BF16), pairs[:, width + 128 * p : width + 128 * p + 128])
        acc.append(jnp.where(low, c[:horizon], c[horizon:]))
        top.append(jnp.where(low, m[:horizon], m[horizon:]))
        total.append(jnp.where(low, s[:horizon], s[horizon:]))
    return jnp.concatenate(acc, 1), jnp.concatenate(top, 1), jnp.concatenate(total, 1)


def encode(context, lse):
    lane = lax.broadcasted_iota(jnp.int32, (lse.shape[0], 128), 1) & 63
    stats = jnp.zeros((lse.shape[0], 128), F32)
    for p in range(lse.shape[1] // 128):
        rest = lse[:, 128 * p : 128 * p + 128]
        for piece in range(3):
            part = rest.astype(BF16).astype(F32)
            stats = jnp.where(lane == 3 * p + piece, part, stats)
            rest = rest - part
    return jnp.concatenate([context.astype(BF16), stats.astype(BF16)], 1)


def spread_matrix(width):
    row = lax.broadcasted_iota(jnp.int32, (128, width), 0)
    col = lax.broadcasted_iota(jnp.int32, (128, width), 1)
    piece = (row & 63) - 3 * (col >> 7)
    return jnp.where((piece >= 0) & (piece < 3) & ((row >> 6) == ((col >> 6) & 1)), 1.0, 0.0).astype(BF16)


def decode(rows, spread):
    width = rows.shape[1] - 128
    return rows[:, :width].astype(F32), dot(rows[:, width:], spread)


def combine(parts):
    top = functools.reduce(jnp.maximum, [l for _, l in parts])
    weights = [jnp.exp(l - top) for _, l in parts]
    total = functools.reduce(jnp.add, weights)
    context = functools.reduce(jnp.add, [w * c for w, (c, _) in zip(weights, parts)])
    return context / total, top + jnp.log(total)


def valid(side):
    here, count = lax.axis_index("tm"), lax.axis_size("tm")
    return jnp.where(here == count - 2 + side, 0.0, 1.0).astype(F32)


def early_kernel(own, got0, got1, near0, near1, taps, gains, up_v, down_v, kv_v, queries, tail, acc, top, total,
                 x0, x1, sem):
    side, series = lax.rem(lax.axis_index("tm"), 2), lax.rem(lax.axis_index("series"), 2)
    pltpu.make_async_copy(own, x0.at[pl.ds(side * 7, 4)], sem.at[0]).start()
    got_at, near_at = pl.ds(4 - side, 4), pl.ds(8 - 8 * side, 3)
    for which, got, near in ((0, got0, near0), (1, got1, near1)):
        @pl.when(series == which)
        def _():
            pltpu.make_async_copy(got, x0.at[got_at], sem.at[1]).start()
            pltpu.make_async_copy(near, x0.at[near_at], sem.at[2]).start()
    v = valid(0)
    one = 1.0
    pltpu.make_async_copy(own, x0.at[pl.ds(side * 7, 4)], sem.at[0]).wait()
    pltpu.make_async_copy(got0, x0.at[got_at], sem.at[1]).wait()
    pltpu.make_async_copy(near0, x0.at[near_at], sem.at[2]).wait()
    rows0 = x0.reshape(11 * HALF, x0.shape[-1])
    for j in range(0, 9, 3):
        factors = [(v, v), (one, v), (one, one)] if j == 6 else [(one, one)] * 3
        x1[j * HALF : (j + 3) * HALF, :] = mix(
            rows0, j + 2, 3, 1, taps[0], gains[0:1, :], up_v[0], down_v[0], factors
        )
    tail[...] = x1[pl.ds(pl.multiple_of(side * (5 * HALF), HALF), 4 * HALF), :]
    x2 = jnp.concatenate([
        mix(x1, 4, 2, 2, taps[1], gains[1:2, :], up_v[1], down_v[1], [(one, one)] * 2),
        mix(x1, 6, 3, 2, taps[1], gains[1:2, :], up_v[1], down_v[1], [(v, v), (v, v), (one, v)]),
    ], 0)
    acc[...], top[...], total[...] = attend(x2, kv_v[...], queries[...])


def late_kernel(own, far0, far1, tail, acc, top, total, taps, gains, up_v, down_v, kv_v, queries, out, x0, x1, sem):
    side, series = lax.rem(lax.axis_index("tm"), 2), lax.rem(lax.axis_index("series"), 2)
    own_copy = pltpu.make_async_copy(own.at[pl.ds(2 * side, 2)], x0.at[pl.ds(3 - 3 * side, 2)], sem.at[0])
    own_copy.start()
    for which, far in ((0, far0), (1, far1)):
        @pl.when(series == which)
        def _():
            pltpu.make_async_copy(far, x0.at[pl.ds(2 * side, 3)], sem.at[1]).start()
    x1[pl.ds(pl.multiple_of((3 - 3 * side) * HALF, HALF), 4 * HALF), :] = tail[...]
    v = valid(1)
    one = 1.0
    own_copy.wait()
    pltpu.make_async_copy(far0, x0.at[pl.ds(2 * side, 3)], sem.at[1]).wait()
    rows0 = x0.reshape(5 * HALF, x0.shape[-1])
    fresh = mix(rows0, 2, 3, 1, taps[0], gains[0:1, :], up_v[0], down_v[0], [(v, v), (one, v), (one, one)])
    x1[pl.ds(pl.multiple_of(side * (4 * HALF), HALF), 3 * HALF), :] = fresh
    x2 = mix(x1, 4, 3, 2, taps[1], gains[1:2, :], up_v[1], down_v[1], [(v, v), (v, v), (one, v)])
    acc2, top2, total2 = attend(x2, kv_v[...], queries[...])
    best = jnp.maximum(top[...], top2)
    a, b = jnp.exp(top[...] - best), jnp.exp(top2 - best)
    whole = total[...] * a + total2 * b
    rows = encode((acc[...] * a + acc2 * b) / whole, best + jnp.log(whole))
    out[...] = rows


def start_all(copies):
    for copy in copies:
        copy.start()
    for copy in copies:
        copy.wait()


def pack_kernel(n, hist, *refs):
    side = lax.rem(lax.axis_index("tm"), 2)
    mine = pl.ds(pl.multiple_of(side * HALF, HALF), HALF)
    other = pl.ds(pl.multiple_of((1 - side) * HALF, HALF), HALF)
    three = pl.ds(side, 3)
    if n == 0:
        out, sem = refs
        start_all([pltpu.make_async_copy(hist.at[:, other, :], out, sem.at[0])])
    elif n == 1:
        near, far, sem = refs
        start_all([
            pltpu.make_async_copy(hist.at[three, mine, :], near, sem.at[0]),
            pltpu.make_async_copy(hist.at[three, other, :], far, sem.at[1]),
        ])
    else:
        whole, (own, *outs, sem) = refs[:4], refs[4:]
        start_all(
            [pltpu.make_async_copy(a, b, sem.at[i]) for i, (a, b) in enumerate(zip(whole, outs))]
            + [pltpu.make_async_copy(hist.at[:, mine, :], own, sem.at[4])]
        )


def final_kernel(parts, readout, out):
    share, width = out.shape
    rows = parts[...]
    context, lse = decode(rows, spread_matrix(width))
    count = rows.shape[0] // share
    cut = [slice(i * share, (i + 1) * share) for i in range(count)]
    context, _ = combine([(context[c], lse[c]) for c in cut])
    out[...] = dot(context.astype(BF16), readout[...]).astype(BF16)


def small(limit=8):
    return pltpu.CompilerParams(vmem_limit_bytes=limit * 1024 * 1024)


def on_device(history, taps, gains, up, down, w_kv, readout, queries):
    _, span, width = history.shape
    horizon, hidden = queries.shape[0], up.shape[-1]
    count = lax.axis_size("tm")
    here = lax.axis_index("tm")
    side, pair = lax.rem(here, 2), lax.div(here, 2)
    n_pairs = count // 2
    share = horizon // count

    hist = history.reshape(span // STEP, STEP, width)
    swap = [(i, i ^ 1) for i in range(count)]
    ahead = [(2 * p + 1, 2 * p + 2) for p in range(n_pairs - 1)]
    behind = [(2 * p, (2 * p - 2) % count) for p in range(n_pairs)]
    near_pairs = [(s, t + 1) for s, t in ahead] + behind
    far_pairs = ahead + [(s, t + 1) for s, t in behind]

    def send(value, *by_series):
        pairs = [
            (r * count + s, r * count + t)
            for r in range(lax.axis_size("series")) for s, t in by_series[r % 2]
        ]
        return lax.ppermute(value, ("series", "tm"), pairs)

    four, three = (jax.ShapeDtypeStruct((k, HALF, width), BF16) for k in (4, 3))
    swap_out = pl.pallas_call(
        functools.partial(pack_kernel, 0),
        out_shape=four,
        in_specs=[HBM],
        out_specs=VMEM,
        scratch_shapes=[pltpu.SemaphoreType.DMA((1,))],
        compiler_params=small(),
        name="pack_swap",
    )(hist)
    got0 = send(swap_out, swap, [])
    near_out, far_out = pl.pallas_call(
        functools.partial(pack_kernel, 1),
        out_shape=[three, three],
        in_specs=[HBM],
        out_specs=[VMEM, VMEM],
        scratch_shapes=[pltpu.SemaphoreType.DMA((2,))],
        compiler_params=small(),
        name="pack_halo",
    )(hist)
    near0 = send(near_out, near_pairs, [])
    own, up_v, down_v, kv_v, readout_v = pl.pallas_call(
        functools.partial(pack_kernel, 2),
        out_shape=[jax.ShapeDtypeStruct((4, HALF, width), BF16)]
        + [jax.ShapeDtypeStruct(w.shape, w.dtype) for w in (up, down, w_kv, readout)],
        in_specs=[HBM] * 5,
        out_specs=[VMEM] * 5,
        scratch_shapes=[pltpu.SemaphoreType.DMA((5,))],
        compiler_params=small(16),
        name="stage",
    )(hist, up, down, w_kv, readout)
    own, swap_out, near_out, far_out = lax.optimization_barrier((own, swap_out, near_out, far_out))
    far0 = send(far_out, far_pairs, [])
    got1 = send(swap_out, [], swap)
    near1 = send(near_out, [], near_pairs)
    far1 = send(far_out, [], far_pairs)
    state = jax.ShapeDtypeStruct((horizon, width), F32)
    per_row = 4 * width * hidden
    tail, acc, top, total = pl.pallas_call(
        early_kernel,
        out_shape=[jax.ShapeDtypeStruct((4 * HALF, width), BF16), state, state, state],
        in_specs=[ANY] * 5 + [VMEM] * 6,
        out_specs=[VMEM] * 4,
        scratch_shapes=[
            pltpu.VMEM((11, HALF, width), BF16), pltpu.VMEM((9 * HALF, width), BF16), pltpu.SemaphoreType.DMA((3,))
        ],
        compiler_params=pltpu.CompilerParams(vmem_limit_bytes=32 * 1024 * 1024),
        cost_estimate=pl.CostEstimate(
            flops=(14 * per_row + 5 * 2 * per_row) * HALF, bytes_accessed=8 << 20, transcendentals=2 << 20
        ),
        name="early",
    )(own, got0, got1, near0, near1, taps, gains, up_v, down_v, kv_v, queries)
    lanes = width + 128
    payload = pl.pallas_call(
        late_kernel,
        out_shape=jax.ShapeDtypeStruct((horizon, lanes), BF16),
        in_specs=[ANY] * 3 + [VMEM] * 10,
        out_specs=VMEM,
        scratch_shapes=[
            pltpu.VMEM((5, HALF, width), BF16), pltpu.VMEM((7 * HALF, width), BF16), pltpu.SemaphoreType.DMA((2,))
        ],
        compiler_params=pltpu.CompilerParams(vmem_limit_bytes=32 * 1024 * 1024),
        cost_estimate=pl.CostEstimate(
            flops=(6 * per_row + 3 * 2 * per_row) * HALF, bytes_accessed=8 << 20, transcendentals=1 << 20
        ),
        name="late",
    )(own, far0, far1, tail, acc, top, total, taps, gains, up_v, down_v, kv_v, queries)
    parts = lax.all_to_all(payload, "tm", 0, 0, tiled=True)
    result = pl.pallas_call(
        final_kernel,
        out_shape=jax.ShapeDtypeStruct((share, width), BF16),
        in_specs=[VMEM] * 2,
        out_specs=VMEM,
        compiler_params=small(),
        name="final",
    )(parts, readout_v)
    return result[None]


def solution(mesh):
    placed = (P(("groups", "series"), "tm", None), P(), P(), P(), P(), P(), P(), P())
    return jax.shard_map(
        on_device,
        mesh=mesh,
        in_specs=placed,
        out_specs=P(("groups", "series"), "tm", None),
        check_vma=False,
    )
```

```python
import functools

import jax
import jax.numpy as jnp
from jax import lax
from jax.experimental import pallas as pl
from jax.experimental.pallas import tpu as pltpu
from jax.sharding import PartitionSpec as P

HEADS = 8
STEP = 256
HALF = STEP // 2
BF16, F32 = jnp.bfloat16, jnp.float32
ANY = pl.BlockSpec(memory_space=pl.ANY)
VMEM = pl.BlockSpec(memory_space=pltpu.VMEM)
HBM = pl.BlockSpec(memory_space=pltpu.HBM)


def dot(a, b):
    return jnp.dot(a, b, preferred_element_type=F32)


def gelu(u):
    half = 0.5 * u
    return half + half * jnp.tanh(u * (0.7978845608028654 + (0.7978845608028654 * 0.044715) * (u * u)))


def mix(src, first, steps, dilation, taps, gain, up, down, factors):
    rows, kept = [], []
    for j in range(steps):
        w1, w2 = factors[j]
        at = [(first + j - k * dilation) * HALF for k in range(3)]
        now = src[at[0] : at[0] + HALF, :].astype(F32)
        conv = taps[0:1, :] * now
        conv = conv + (taps[1:2, :] * w1) * src[at[1] : at[1] + HALF, :].astype(F32)
        conv = conv + (taps[2:3, :] * w2) * src[at[2] : at[2] + HALF, :].astype(F32)
        scale = lax.rsqrt(jnp.mean(conv * conv, axis=-1, keepdims=True) + 1e-05)
        rows.append((conv * scale * gain).astype(BF16))
        kept.append(now)
    inner = gelu(dot(jnp.concatenate(rows, 0), up)).astype(BF16)
    return (jnp.concatenate(kept, 0) + dot(inner, down)).astype(BF16)


def attend(x2, w_kv, queries):
    pairs = dot(x2, w_kv).astype(BF16)
    horizon, width = queries.shape
    low = lax.broadcasted_iota(jnp.int32, (horizon, 128), 1) < 64
    zero = jnp.zeros((horizon, 128), BF16)
    acc, top, total, scores = [], [], [], []
    for p in range(width // 128):
        lanes = slice(128 * p, 128 * p + 128)
        q = queries[:, lanes] * jnp.asarray(0.125, BF16)
        q2 = jnp.concatenate([jnp.where(low, q, zero), jnp.where(low, zero, q)], 0)
        scores.append(
            lax.dot_general(q2, pairs[:, lanes], (((1,), (1,)), ((), ())), preferred_element_type=F32)
        )
    for p in range(width // 128):
        m = jnp.max(scores[p], axis=-1, keepdims=True)
        e = jnp.exp(scores[p] - m)
        s = jnp.sum(e, axis=-1, keepdims=True)
        c = dot(e.astype(BF16), pairs[:, width + 128 * p : width + 128 * p + 128])
        acc.append(jnp.where(low, c[:horizon], c[horizon:]))
        top.append(jnp.where(low, m[:horizon], m[horizon:]))
        total.append(jnp.where(low, s[:horizon], s[horizon:]))
    return jnp.concatenate(acc, 1), jnp.concatenate(top, 1), jnp.concatenate(total, 1)


def encode(context, lse):
    lane = lax.broadcasted_iota(jnp.int32, (lse.shape[0], 128), 1) & 63
    stats = jnp.zeros((lse.shape[0], 128), F32)
    for p in range(lse.shape[1] // 128):
        rest = lse[:, 128 * p : 128 * p + 128]
        for piece in range(3):
            part = rest.astype(BF16).astype(F32)
            stats = jnp.where(lane == 3 * p + piece, part, stats)
            rest = rest - part
    return jnp.concatenate([context.astype(BF16), stats.astype(BF16)], 1)


def spread_matrix(width):
    row = lax.broadcasted_iota(jnp.int32, (128, width), 0)
    col = lax.broadcasted_iota(jnp.int32, (128, width), 1)
    piece = (row & 63) - 3 * (col >> 7)
    return jnp.where((piece >= 0) & (piece < 3) & ((row >> 6) == ((col >> 6) & 1)), 1.0, 0.0).astype(BF16)


def decode(rows, spread):
    width = rows.shape[1] - 128
    return rows[:, :width].astype(F32), dot(rows[:, width:], spread)


def combine(parts):
    top = functools.reduce(jnp.maximum, [l for _, l in parts])
    weights = [jnp.exp(l - top) for _, l in parts]
    total = functools.reduce(jnp.add, weights)
    context = functools.reduce(jnp.add, [w * c for w, (c, _) in zip(weights, parts)])
    return context / total, top + jnp.log(total)


def valid(side):
    here, count = lax.axis_index("tm"), lax.axis_size("tm")
    return jnp.where(here == count - 2 + side, 0.0, 1.0).astype(F32)


def early_kernel(own, got, near, taps, gains, up_v, down_v, kv_v, queries, tail, acc, top, total,
                 x0, x1, sem):
    side = lax.rem(lax.axis_index("tm"), 2)
    copies = [
        pltpu.make_async_copy(own, x0.at[pl.ds(side * 7, 4)], sem.at[0]),
        pltpu.make_async_copy(got, x0.at[pl.ds(4 - side, 4)], sem.at[1]),
        pltpu.make_async_copy(near, x0.at[pl.ds(8 - 8 * side, 3)], sem.at[2]),
    ]
    for copy in copies:
        copy.start()
    v = valid(0)
    one = 1.0
    for copy in copies:
        copy.wait()
    rows0 = x0.reshape(11 * HALF, x0.shape[-1])
    for j in range(0, 9, 3):
        factors = [(v, v), (one, v), (one, one)] if j == 6 else [(one, one)] * 3
        x1[j * HALF : (j + 3) * HALF, :] = mix(
            rows0, j + 2, 3, 1, taps[0], gains[0:1, :], up_v[0], down_v[0], factors
        )
    tail[...] = x1[pl.ds(pl.multiple_of(side * (5 * HALF), HALF), 4 * HALF), :]
    x2 = jnp.concatenate([
        mix(x1, 4, 2, 2, taps[1], gains[1:2, :], up_v[1], down_v[1], [(one, one)] * 2),
        mix(x1, 6, 3, 2, taps[1], gains[1:2, :], up_v[1], down_v[1], [(v, v), (v, v), (one, v)]),
    ], 0)
    acc[...], top[...], total[...] = attend(x2, kv_v[...], queries[...])


def late_kernel(own, far, tail, acc, top, total, taps, gains, up_v, down_v, kv_v, queries, out, x0, x1, sem):
    side = lax.rem(lax.axis_index("tm"), 2)
    copies = [
        pltpu.make_async_copy(own.at[pl.ds(2 * side, 2)], x0.at[pl.ds(3 - 3 * side, 2)], sem.at[0]),
        pltpu.make_async_copy(far, x0.at[pl.ds(2 * side, 3)], sem.at[1]),
    ]
    for copy in copies:
        copy.start()
    x1[pl.ds(pl.multiple_of((3 - 3 * side) * HALF, HALF), 4 * HALF), :] = tail[...]
    v = valid(1)
    one = 1.0
    for copy in copies:
        copy.wait()
    rows0 = x0.reshape(5 * HALF, x0.shape[-1])
    fresh = mix(rows0, 2, 3, 1, taps[0], gains[0:1, :], up_v[0], down_v[0], [(v, v), (one, v), (one, one)])
    x1[pl.ds(pl.multiple_of(side * (4 * HALF), HALF), 3 * HALF), :] = fresh
    x2 = mix(x1, 4, 3, 2, taps[1], gains[1:2, :], up_v[1], down_v[1], [(v, v), (v, v), (one, v)])
    acc2, top2, total2 = attend(x2, kv_v[...], queries[...])
    best = jnp.maximum(top[...], top2)
    a, b = jnp.exp(top[...] - best), jnp.exp(top2 - best)
    whole = total[...] * a + total2 * b
    rows = encode((acc[...] * a + acc2 * b) / whole, best + jnp.log(whole))
    out[...] = rows


def pack_kernel(n, hist, *refs):
    side = lax.rem(lax.axis_index("tm"), 2)
    mine = pl.ds(pl.multiple_of(side * HALF, HALF), HALF)
    other = pl.ds(pl.multiple_of((1 - side) * HALF, HALF), HALF)
    three = pl.ds(side, 3)
    if n == 0:
        swap_out, sem = refs
        copies = [pltpu.make_async_copy(hist.at[:, other, :], swap_out, sem.at[0])]
    elif n == 2:
        whole, (own_out, *outs, sem) = refs[:4], refs[4:]
        copies = [
            pltpu.make_async_copy(a, b, sem.at[i]) for i, (a, b) in enumerate(zip(whole, outs))
        ] + [pltpu.make_async_copy(hist.at[:, mine, :], own_out, sem.at[4])]
    else:
        near_out, far_out, sem = refs
        copies = [
            pltpu.make_async_copy(hist.at[three, mine, :], near_out, sem.at[0]),
            pltpu.make_async_copy(hist.at[three, other, :], far_out, sem.at[1]),
        ]
    for copy in copies:
        copy.start()
    for copy in copies:
        copy.wait()


def final_kernel(parts, readout, out):
    share, width = out.shape
    rows = parts[...]
    context, lse = decode(rows, spread_matrix(width))
    count = rows.shape[0] // share
    cut = [slice(i * share, (i + 1) * share) for i in range(count)]
    context, _ = combine([(context[c], lse[c]) for c in cut])
    out[...] = dot(context.astype(BF16), readout[...]).astype(BF16)


def small(limit=8):
    return pltpu.CompilerParams(vmem_limit_bytes=limit * 1024 * 1024)


def on_device(history, taps, gains, up, down, w_kv, readout, queries):
    _, span, width = history.shape
    horizon, hidden = queries.shape[0], up.shape[-1]
    count = lax.axis_size("tm")
    n_pairs = count // 2
    share = horizon // count

    hist = history.reshape(span // STEP, STEP, width)
    swap = [(i, i ^ 1) for i in range(count)]
    ahead = [(2 * p + 1, 2 * p + 2) for p in range(n_pairs - 1)]
    behind = [(2 * p, (2 * p - 2) % count) for p in range(n_pairs)]
    near_pairs = [(s, t + 1) for s, t in ahead] + behind
    far_pairs = ahead + [(s, t + 1) for s, t in behind]
    three = jax.ShapeDtypeStruct((3, HALF, width), BF16)
    swap_out = pl.pallas_call(
        functools.partial(pack_kernel, 0),
        out_shape=jax.ShapeDtypeStruct((4, HALF, width), BF16),
        in_specs=[HBM],
        out_specs=VMEM,
        scratch_shapes=[pltpu.SemaphoreType.DMA((1,))],
        compiler_params=small(),
        name="pack_swap",
    )(hist)
    got = lax.ppermute(swap_out, "tm", swap)
    near_out, far_out = pl.pallas_call(
        functools.partial(pack_kernel, 1),
        out_shape=[three, three],
        in_specs=[HBM],
        out_specs=[VMEM, VMEM],
        scratch_shapes=[pltpu.SemaphoreType.DMA((2,))],
        compiler_params=small(),
        name="pack_halo",
    )(hist)
    near = lax.ppermute(near_out, "tm", near_pairs)
    far = lax.ppermute(far_out, "tm", far_pairs)

    own, up_v, down_v, kv_v, readout_v = pl.pallas_call(
        functools.partial(pack_kernel, 2),
        out_shape=[jax.ShapeDtypeStruct((4, HALF, width), BF16)]
        + [jax.ShapeDtypeStruct(w.shape, w.dtype) for w in (up, down, w_kv, readout)],
        in_specs=[HBM] * 5,
        out_specs=[VMEM] * 5,
        scratch_shapes=[pltpu.SemaphoreType.DMA((5,))],
        compiler_params=small(16),
        name="stage",
    )(hist, up, down, w_kv, readout)
    state = jax.ShapeDtypeStruct((horizon, width), F32)
    per_row = 4 * width * hidden
    tail, acc, top, total = pl.pallas_call(
        early_kernel,
        out_shape=[jax.ShapeDtypeStruct((4 * HALF, width), BF16), state, state, state],
        in_specs=[ANY] * 3 + [VMEM] * 6,
        out_specs=[VMEM] * 4,
        scratch_shapes=[
            pltpu.VMEM((11, HALF, width), BF16), pltpu.VMEM((9 * HALF, width), BF16), pltpu.SemaphoreType.DMA((3,))
        ],
        compiler_params=pltpu.CompilerParams(vmem_limit_bytes=32 * 1024 * 1024),
        cost_estimate=pl.CostEstimate(
            flops=(14 * per_row + 5 * 2 * per_row) * HALF, bytes_accessed=8 << 20, transcendentals=2 << 20
        ),
        name="early",
    )(own, got, near, taps, gains, up_v, down_v, kv_v, queries)
    lanes = width + 128
    payload = pl.pallas_call(
        late_kernel,
        out_shape=jax.ShapeDtypeStruct((horizon, lanes), BF16),
        in_specs=[ANY] * 2 + [VMEM] * 10,
        out_specs=VMEM,
        scratch_shapes=[
            pltpu.VMEM((5, HALF, width), BF16), pltpu.VMEM((7 * HALF, width), BF16), pltpu.SemaphoreType.DMA((2,))
        ],
        compiler_params=pltpu.CompilerParams(vmem_limit_bytes=32 * 1024 * 1024),
        cost_estimate=pl.CostEstimate(
            flops=(6 * per_row + 3 * 2 * per_row) * HALF, bytes_accessed=8 << 20, transcendentals=1 << 20
        ),
        name="late",
    )(own, far, tail, acc, top, total, taps, gains, up_v, down_v, kv_v, queries)
    parts = lax.all_to_all(payload, "tm", 0, 0, tiled=True)
    result = pl.pallas_call(
        final_kernel,
        out_shape=jax.ShapeDtypeStruct((share, width), BF16),
        in_specs=[VMEM] * 2,
        out_specs=VMEM,
        compiler_params=small(),
        name="final",
    )(parts, readout_v)
    return result[None]


def solution(mesh):
    placed = (P(("groups", "series"), "tm", None), P(), P(), P(), P(), P(), P(), P())
    return jax.shard_map(
        on_device,
        mesh=mesh,
        in_specs=placed,
        out_specs=P(("groups", "series"), "tm", None),
        check_vma=False,
    )
```

```python
import functools

import jax
import jax.numpy as jnp
from jax import lax
from jax.experimental import pallas as pl
from jax.experimental.pallas import tpu as pltpu
from jax.sharding import PartitionSpec as P

HEADS = 8
STEP = 256
HALF = STEP // 2
BF16, F32 = jnp.bfloat16, jnp.float32
ANY = pl.BlockSpec(memory_space=pl.ANY)
VMEM = pl.BlockSpec(memory_space=pltpu.VMEM)
HBM = pl.BlockSpec(memory_space=pltpu.HBM)


def dot(a, b):
    return jnp.dot(a, b, preferred_element_type=F32)


def gelu(u):
    half = 0.5 * u
    return half + half * jnp.tanh(u * (0.7978845608028654 + (0.7978845608028654 * 0.044715) * (u * u)))


def mix(src, first, steps, dilation, taps, gain, up, down, reach=None):
    rows, kept = [], []
    for j in range(steps):
        conv = None
        for k in range(reach[j] if reach else 3):
            at = (first + j - k * dilation) * HALF
            value = src[at : at + HALF, :].astype(F32)
            if k == 0:
                kept.append(value)
            conv = taps[k : k + 1, :] * value if k == 0 else conv + taps[k : k + 1, :] * value
        scale = lax.rsqrt(jnp.mean(conv * conv, axis=-1, keepdims=True) + 1e-05)
        rows.append((conv * scale * gain).astype(BF16))
    inner = gelu(dot(jnp.concatenate(rows, 0), up)).astype(BF16)
    return (jnp.concatenate(kept, 0) + dot(inner, down)).astype(BF16)


def attend(x2, w_kv, queries, absent=None):
    pairs = dot(x2, w_kv).astype(BF16)
    horizon, width = queries.shape
    low = lax.broadcasted_iota(jnp.int32, (horizon, 128), 1) < 64
    zero = jnp.zeros((horizon, 128), BF16)
    acc, top, total, scores = [], [], [], []
    for p in range(width // 128):
        lanes = slice(128 * p, 128 * p + 128)
        q = queries[:, lanes] * jnp.asarray(0.125, BF16)
        q2 = jnp.concatenate([jnp.where(low, q, zero), jnp.where(low, zero, q)], 0)
        scores.append(
            lax.dot_general(q2, pairs[:, lanes], (((1,), (1,)), ((), ())), preferred_element_type=F32)
        )
    if absent is not None:
        row = lax.broadcasted_iota(jnp.int32, (1, x2.shape[0]), 1)
        bias = jnp.where(row < absent, 0.0, -1e30).astype(F32)
        scores = [s + bias for s in scores]
    for p in range(width // 128):
        m = jnp.max(scores[p], axis=-1, keepdims=True)
        e = jnp.exp(scores[p] - m)
        s = jnp.sum(e, axis=-1, keepdims=True)
        c = dot(e.astype(BF16), pairs[:, width + 128 * p : width + 128 * p + 128])
        acc.append(jnp.where(low, c[:horizon], c[horizon:]))
        top.append(jnp.where(low, m[:horizon], m[horizon:]))
        total.append(jnp.where(low, s[:horizon], s[horizon:]))
    return jnp.concatenate(acc, 1), jnp.concatenate(top, 1), jnp.concatenate(total, 1)


def encode(context, lse):
    lane = lax.broadcasted_iota(jnp.int32, (lse.shape[0], 128), 1) & 63
    stats = jnp.zeros((lse.shape[0], 128), F32)
    for p in range(lse.shape[1] // 128):
        rest = lse[:, 128 * p : 128 * p + 128]
        for piece in range(3):
            part = rest.astype(BF16).astype(F32)
            stats = jnp.where(lane == 3 * p + piece, part, stats)
            rest = rest - part
    return jnp.concatenate([context.astype(BF16), stats.astype(BF16)], 1)


def spread_matrix(width):
    row = lax.broadcasted_iota(jnp.int32, (128, width), 0)
    col = lax.broadcasted_iota(jnp.int32, (128, width), 1)
    piece = (row & 63) - 3 * (col >> 7)
    return jnp.where((piece >= 0) & (piece < 3) & ((row >> 6) == ((col >> 6) & 1)), 1.0, 0.0).astype(BF16)


def decode(rows, spread):
    width = rows.shape[1] - 128
    return rows[:, :width].astype(F32), dot(rows[:, width:], spread)


def combine(parts):
    top = functools.reduce(jnp.maximum, [l for _, l in parts])
    weights = [jnp.exp(l - top) for _, l in parts]
    total = functools.reduce(jnp.add, weights)
    context = functools.reduce(jnp.add, [w * c for w, (c, _) in zip(weights, parts)])
    return context / total, top + jnp.log(total)


def join(a, b):
    best = jnp.maximum(a[1], b[1])
    wa, wb = jnp.exp(a[1] - best), jnp.exp(b[1] - best)
    return a[0] * wa + b[0] * wb, best, a[2] * wa + b[2] * wb


def first_steps(x1, taps, gains, up_v, down_v, kv_v, queries, state):
    x2 = mix(x1, 1, 3, 2, taps[1], gains[1:2, :], up_v[1], down_v[1], (1, 1, 2))
    added = join([ref[...] for ref in state], attend(x2, kv_v[...], queries[...]))
    for ref, value in zip(state, added):
        ref[...] = value


def early_kernel(own, got, near, taps, gains, up_v, down_v, kv_v, queries, tail, acc, top, total,
                 x0, x1, sem):
    side = lax.rem(lax.axis_index("tm"), 2)
    copies = [
        pltpu.make_async_copy(own, x0.at[pl.ds(side * 7, 4)], sem.at[0]),
        pltpu.make_async_copy(got, x0.at[pl.ds(4 - side, 4)], sem.at[1]),
        pltpu.make_async_copy(near, x0.at[pl.ds(8 - 8 * side, 3)], sem.at[2]),
    ]
    for copy in copies:
        copy.start()
    for copy in copies:
        copy.wait()
    rows0 = x0.reshape(11 * HALF, x0.shape[-1])
    for j in range(0, 9, 3):
        x1[j * HALF : (j + 3) * HALF, :] = mix(rows0, j + 2, 3, 1, taps[0], gains[0:1, :], up_v[0], down_v[0])
    tail[...] = x1[pl.ds(pl.multiple_of(side * (5 * HALF), HALF), 4 * HALF), :]
    x2 = jnp.concatenate([
        mix(x1, 4, 2, 2, taps[1], gains[1:2, :], up_v[1], down_v[1]),
        mix(x1, 6, 3, 2, taps[1], gains[1:2, :], up_v[1], down_v[1]),
    ], 0)
    here, count = lax.axis_index("tm"), lax.axis_size("tm")
    absent = jnp.where(here == count - 2, 2 * HALF, 5 * HALF)
    acc[...], top[...], total[...] = attend(x2, kv_v[...], queries[...], absent)

    @pl.when(here == 1)
    def _():
        first_steps(x1, taps, gains, up_v, down_v, kv_v, queries, (acc, top, total))


def late_kernel(own, far, tail, acc, top, total, taps, gains, up_v, down_v, kv_v, queries, out, x0, x1, acc2, top2, total2, sem):
    side = lax.rem(lax.axis_index("tm"), 2)
    copies = [
        pltpu.make_async_copy(own.at[pl.ds(2 * side, 2)], x0.at[pl.ds(3 - 3 * side, 2)], sem.at[0]),
        pltpu.make_async_copy(far, x0.at[pl.ds(2 * side, 3)], sem.at[1]),
    ]
    for copy in copies:
        copy.start()
    x1[pl.ds(pl.multiple_of((3 - 3 * side) * HALF, HALF), 4 * HALF), :] = tail[...]
    for copy in copies:
        copy.wait()
    rows0 = x0.reshape(5 * HALF, x0.shape[-1])
    fresh = mix(rows0, 2, 3, 1, taps[0], gains[0:1, :], up_v[0], down_v[0])
    x1[pl.ds(pl.multiple_of(side * (4 * HALF), HALF), 3 * HALF), :] = fresh
    x2 = mix(x1, 4, 3, 2, taps[1], gains[1:2, :], up_v[1], down_v[1])
    here, count = lax.axis_index("tm"), lax.axis_size("tm")
    absent = jnp.where(here == count - 1, 0, 3 * HALF)
    acc2[...], top2[...], total2[...] = join(
        (acc[...], top[...], total[...]), attend(x2, kv_v[...], queries[...], absent)
    )

    @pl.when(here == 0)
    def _():
        first_steps(x1, taps, gains, up_v, down_v, kv_v, queries, (acc2, top2, total2))

    out[...] = encode(acc2[...] / total2[...], top2[...] + jnp.log(total2[...]))


def pack_kernel(n, hist, *refs):
    side = lax.rem(lax.axis_index("tm"), 2)
    mine = pl.ds(pl.multiple_of(side * HALF, HALF), HALF)
    other = pl.ds(pl.multiple_of((1 - side) * HALF, HALF), HALF)
    three = pl.ds(side, 3)
    if n == 0:
        swap_out, sem = refs
        copies = [pltpu.make_async_copy(hist.at[:, other, :], swap_out, sem.at[0])]
    elif n == 2:
        whole, (own_out, *outs, sem) = refs[:4], refs[4:]
        copies = [
            pltpu.make_async_copy(a, b, sem.at[i]) for i, (a, b) in enumerate(zip(whole, outs))
        ] + [pltpu.make_async_copy(hist.at[:, mine, :], own_out, sem.at[4])]
    else:
        near_out, far_out, sem = refs
        copies = [
            pltpu.make_async_copy(hist.at[three, mine, :], near_out, sem.at[0]),
            pltpu.make_async_copy(hist.at[three, other, :], far_out, sem.at[1]),
        ]
    for copy in copies:
        copy.start()
    for copy in copies:
        copy.wait()


def final_kernel(parts, readout, out):
    share, width = out.shape
    rows = parts[...]
    context, lse = decode(rows, spread_matrix(width))
    count = rows.shape[0] // share
    cut = [slice(i * share, (i + 1) * share) for i in range(count)]
    context, _ = combine([(context[c], lse[c]) for c in cut])
    out[...] = dot(context.astype(BF16), readout[...]).astype(BF16)


def small(limit=8):
    return pltpu.CompilerParams(vmem_limit_bytes=limit * 1024 * 1024)


def on_device(history, taps, gains, up, down, w_kv, readout, queries):
    _, span, width = history.shape
    horizon, hidden = queries.shape[0], up.shape[-1]
    count = lax.axis_size("tm")
    n_pairs = count // 2
    share = horizon // count

    hist = history.reshape(span // STEP, STEP, width)
    swap = [(i, i ^ 1) for i in range(count)]
    ahead = [(2 * p + 1, 2 * p + 2) for p in range(n_pairs - 1)]
    behind = [(2 * p, 2 * p - 2) for p in range(1, n_pairs)]
    near_pairs = [(s, t + 1) for s, t in ahead] + behind
    far_pairs = ahead + [(s, t + 1) for s, t in behind]
    three = jax.ShapeDtypeStruct((3, HALF, width), BF16)
    swap_out = pl.pallas_call(
        functools.partial(pack_kernel, 0),
        out_shape=jax.ShapeDtypeStruct((4, HALF, width), BF16),
        in_specs=[HBM],
        out_specs=VMEM,
        scratch_shapes=[pltpu.SemaphoreType.DMA((1,))],
        compiler_params=small(),
        name="pack_swap",
    )(hist)
    got = lax.ppermute(swap_out, "tm", swap)
    near_out, far_out = pl.pallas_call(
        functools.partial(pack_kernel, 1),
        out_shape=[three, three],
        in_specs=[HBM],
        out_specs=[VMEM, VMEM],
        scratch_shapes=[pltpu.SemaphoreType.DMA((2,))],
        compiler_params=small(),
        name="pack_halo",
    )(hist)
    near = lax.ppermute(near_out, "tm", near_pairs)
    far = lax.ppermute(far_out, "tm", far_pairs)

    own, up_v, down_v, kv_v, readout_v = pl.pallas_call(
        functools.partial(pack_kernel, 2),
        out_shape=[jax.ShapeDtypeStruct((4, HALF, width), BF16)]
        + [jax.ShapeDtypeStruct(w.shape, w.dtype) for w in (up, down, w_kv, readout)],
        in_specs=[HBM] * 5,
        out_specs=[VMEM] * 5,
        scratch_shapes=[pltpu.SemaphoreType.DMA((5,))],
        compiler_params=small(16),
        name="stage",
    )(hist, up, down, w_kv, readout)
    state = jax.ShapeDtypeStruct((horizon, width), F32)
    per_row = 4 * width * hidden
    tail, acc, top, total = pl.pallas_call(
        early_kernel,
        out_shape=[jax.ShapeDtypeStruct((4 * HALF, width), BF16), state, state, state],
        in_specs=[ANY] * 3 + [VMEM] * 6,
        out_specs=[VMEM] * 4,
        scratch_shapes=[
            pltpu.VMEM((11, HALF, width), BF16), pltpu.VMEM((9 * HALF, width), BF16), pltpu.SemaphoreType.DMA((3,))
        ],
        compiler_params=pltpu.CompilerParams(vmem_limit_bytes=32 * 1024 * 1024),
        cost_estimate=pl.CostEstimate(
            flops=(14 * per_row + 5 * 2 * per_row) * HALF, bytes_accessed=8 << 20, transcendentals=2 << 20
        ),
        name="early",
    )(own, got, near, taps, gains, up_v, down_v, kv_v, queries)
    lanes = width + 128
    payload = pl.pallas_call(
        late_kernel,
        out_shape=jax.ShapeDtypeStruct((horizon, lanes), BF16),
        in_specs=[ANY] * 2 + [VMEM] * 10,
        out_specs=VMEM,
        scratch_shapes=[
            pltpu.VMEM((5, HALF, width), BF16), pltpu.VMEM((7 * HALF, width), BF16),
            *[pltpu.VMEM(state.shape, F32)] * 3, pltpu.SemaphoreType.DMA((2,))
        ],
        compiler_params=pltpu.CompilerParams(vmem_limit_bytes=32 * 1024 * 1024),
        cost_estimate=pl.CostEstimate(
            flops=(6 * per_row + 3 * 2 * per_row) * HALF, bytes_accessed=8 << 20, transcendentals=1 << 20
        ),
        name="late",
    )(own, far, tail, acc, top, total, taps, gains, up_v, down_v, kv_v, queries)
    parts = lax.all_to_all(payload, "tm", 0, 0, tiled=True)
    result = pl.pallas_call(
        final_kernel,
        out_shape=jax.ShapeDtypeStruct((share, width), BF16),
        in_specs=[VMEM] * 2,
        out_specs=VMEM,
        compiler_params=small(),
        name="final",
    )(parts, readout_v)
    return result[None]


def solution(mesh):
    placed = (P(("groups", "series"), "tm", None), P(), P(), P(), P(), P(), P(), P())
    return jax.shard_map(
        on_device,
        mesh=mesh,
        in_specs=placed,
        out_specs=P(("groups", "series"), "tm", None),
        check_vma=False,
    )
```

```python
import functools

import jax
import jax.numpy as jnp
from jax import lax
from jax.experimental import pallas as pl
from jax.experimental.pallas import tpu as pltpu
from jax.sharding import PartitionSpec as P

HEADS = 8
STEP = 256
HALF = STEP // 2
BF16, F32 = jnp.bfloat16, jnp.float32
VMEM = pl.BlockSpec(memory_space=pltpu.VMEM)
HBM = pl.BlockSpec(memory_space=pltpu.HBM)


def dot(a, b):
    return jnp.dot(a, b, preferred_element_type=F32)


def gelu(u):
    half = 0.5 * u
    return half + half * jnp.tanh(u * (0.7978845608028654 + (0.7978845608028654 * 0.044715) * (u * u)))


def groups(ref):
    return lambda g: ref[g * HALF : (g + 1) * HALF, :]


def chain(*refs):
    at = [(ref, g) for ref in refs for g in range(ref.shape[0])]
    return lambda g: at[g][0][at[g][1]]


def mix(get, first, steps, dilation, taps, gain, up, down, reach=None):
    rows, kept = [], []
    for j in range(steps):
        conv = None
        for k in range(reach[j] if reach else 3):
            value = get(first + j - k * dilation).astype(F32)
            if k == 0:
                kept.append(value)
            conv = taps[k : k + 1, :] * value if k == 0 else conv + taps[k : k + 1, :] * value
        scale = lax.rsqrt(jnp.mean(conv * conv, axis=-1, keepdims=True) + 1e-05)
        rows.append((conv * scale * gain).astype(BF16))
    inner = gelu(dot(jnp.concatenate(rows, 0), up)).astype(BF16)
    return (jnp.concatenate(kept, 0) + dot(inner, down)).astype(BF16)


def attend(x2, w_kv, queries, absent=None):
    pairs = dot(x2, w_kv).astype(BF16)
    horizon, width = queries.shape
    low = lax.broadcasted_iota(jnp.int32, (horizon, 128), 1) < 64
    zero = jnp.zeros((horizon, 128), BF16)
    acc, top, total, scores = [], [], [], []
    for p in range(width // 128):
        lanes = slice(128 * p, 128 * p + 128)
        q = queries[:, lanes] * jnp.asarray(0.125, BF16)
        q2 = jnp.concatenate([jnp.where(low, q, zero), jnp.where(low, zero, q)], 0)
        scores.append(
            lax.dot_general(q2, pairs[:, lanes], (((1,), (1,)), ((), ())), preferred_element_type=F32)
        )
    if absent is not None:
        row = lax.broadcasted_iota(jnp.int32, (1, x2.shape[0]), 1)
        bias = jnp.where(row < absent, 0.0, -1e30).astype(F32)
        scores = [s + bias for s in scores]
    for p in range(width // 128):
        m = jnp.max(scores[p], axis=-1, keepdims=True)
        e = jnp.exp(scores[p] - m)
        s = jnp.sum(e, axis=-1, keepdims=True)
        c = dot(e.astype(BF16), pairs[:, width + 128 * p : width + 128 * p + 128])
        acc.append(jnp.where(low, c[:horizon], c[horizon:]))
        top.append(jnp.where(low, m[:horizon], m[horizon:]))
        total.append(jnp.where(low, s[:horizon], s[horizon:]))
    return jnp.concatenate(acc, 1), jnp.concatenate(top, 1), jnp.concatenate(total, 1)


def encode(context, lse):
    lane = lax.broadcasted_iota(jnp.int32, (lse.shape[0], 128), 1) & 63
    stats = jnp.zeros((lse.shape[0], 128), F32)
    for p in range(lse.shape[1] // 128):
        rest = lse[:, 128 * p : 128 * p + 128]
        for piece in range(3):
            part = rest.astype(BF16).astype(F32)
            stats = jnp.where(lane == 3 * p + piece, part, stats)
            rest = rest - part
    return jnp.concatenate([context.astype(BF16), stats.astype(BF16)], 1)


def spread_matrix(width):
    row = lax.broadcasted_iota(jnp.int32, (128, width), 0)
    col = lax.broadcasted_iota(jnp.int32, (128, width), 1)
    piece = (row & 63) - 3 * (col >> 7)
    return jnp.where((piece >= 0) & (piece < 3) & ((row >> 6) == ((col >> 6) & 1)), 1.0, 0.0).astype(BF16)


def decode(rows, spread):
    width = rows.shape[1] - 128
    return rows[:, :width].astype(F32), dot(rows[:, width:], spread)


def combine(parts):
    top = functools.reduce(jnp.maximum, [l for _, l in parts])
    weights = [jnp.exp(l - top) for _, l in parts]
    total = functools.reduce(jnp.add, weights)
    context = functools.reduce(jnp.add, [w * c for w, (c, _) in zip(weights, parts)])
    return context / total, top + jnp.log(total)


def join(a, b):
    best = jnp.maximum(a[1], b[1])
    wa, wb = jnp.exp(a[1] - best), jnp.exp(b[1] - best)
    return a[0] * wa + b[0] * wb, best, a[2] * wa + b[2] * wb


def first_steps(x1, taps, gains, up_v, down_v, kv_v, queries, state):
    x2 = mix(groups(x1), 1, 3, 2, taps[1], gains[1:2, :], up_v[1], down_v[1], (1, 1, 2))
    added = join([ref[...] for ref in state], attend(x2, kv_v[...], queries[...]))
    for ref, value in zip(state, added):
        ref[...] = value


def own_kernel(own, taps, gains, up_v, down_v, out):
    out[...] = mix(chain(own), 2, 2, 1, taps[0], gains[0:1, :], up_v[0], down_v[0])


def early_kernel(own, got, near, done, taps, gains, up_v, down_v, kv_v, queries, tail, acc, top, total, x1):
    here, count = lax.axis_index("tm"), lax.axis_size("tm")

    def block_one(refs, first, done_at, tail_at):
        x1[done_at * HALF : (done_at + 2) * HALF, :] = done[...]
        for j, steps in ((first, 4), (first + 4, 3)):
            x1[j * HALF : (j + steps) * HALF, :] = mix(
                chain(*refs), j + 2, steps, 1, taps[0], gains[0:1, :], up_v[0], down_v[0]
            )
        tail[...] = x1[tail_at * HALF : (tail_at + 4) * HALF, :]

    @pl.when(lax.rem(here, 2) == 0)
    def _():
        block_one((own, got, near), 2, 0, 0)

    @pl.when(lax.rem(here, 2) == 1)
    def _():
        block_one((near, got, own), 0, 7, 5)

    x2 = jnp.concatenate([
        mix(groups(x1), 4, 2, 2, taps[1], gains[1:2, :], up_v[1], down_v[1]),
        mix(groups(x1), 6, 3, 2, taps[1], gains[1:2, :], up_v[1], down_v[1]),
    ], 0)
    absent = jnp.where(here == count - 2, 2 * HALF, 5 * HALF)
    acc[...], top[...], total[...] = attend(x2, kv_v[...], queries[...], absent)

    @pl.when(here == 1)
    def _():
        first_steps(x1, taps, gains, up_v, down_v, kv_v, queries, (acc, top, total))


def late_kernel(own, far, tail, acc, top, total, taps, gains, up_v, down_v, kv_v, queries, out, x1, acc2, top2, total2):
    here, count = lax.axis_index("tm"), lax.axis_size("tm")

    def block_one(refs, new_at, tail_at):
        x1[tail_at * HALF : (tail_at + 4) * HALF, :] = tail[...]
        x1[new_at * HALF : (new_at + 3) * HALF, :] = mix(
            chain(*refs), 2, 3, 1, taps[0], gains[0:1, :], up_v[0], down_v[0]
        )

    @pl.when(lax.rem(here, 2) == 0)
    def _():
        block_one((far, own.at[0:2]), 0, 3)

    @pl.when(lax.rem(here, 2) == 1)
    def _():
        block_one((own.at[2:4], far), 4, 0)

    x2 = mix(groups(x1), 4, 3, 2, taps[1], gains[1:2, :], up_v[1], down_v[1])
    absent = jnp.where(here == count - 1, 0, 3 * HALF)
    acc2[...], top2[...], total2[...] = join(
        (acc[...], top[...], total[...]), attend(x2, kv_v[...], queries[...], absent)
    )

    @pl.when(here == 0)
    def _():
        first_steps(x1, taps, gains, up_v, down_v, kv_v, queries, (acc2, top2, total2))

    out[...] = encode(acc2[...] / total2[...], top2[...] + jnp.log(total2[...]))


def pack_kernel(n, hist, *refs):
    side = lax.rem(lax.axis_index("tm"), 2)
    mine = pl.ds(pl.multiple_of(side * HALF, HALF), HALF)
    other = pl.ds(pl.multiple_of((1 - side) * HALF, HALF), HALF)
    three = pl.ds(side, 3)
    if n == 0:
        swap_out, sem = refs
        copies = [pltpu.make_async_copy(hist.at[:, other, :], swap_out, sem.at[0])]
    elif n == 2:
        whole, (own_out, *outs, sem) = refs[:4], refs[4:]
        copies = [
            pltpu.make_async_copy(a, b, sem.at[i]) for i, (a, b) in enumerate(zip(whole, outs))
        ] + [pltpu.make_async_copy(hist.at[:, mine, :], own_out, sem.at[4])]
    else:
        near_out, far_out, sem = refs
        copies = [
            pltpu.make_async_copy(hist.at[three, mine, :], near_out, sem.at[0]),
            pltpu.make_async_copy(hist.at[three, other, :], far_out, sem.at[1]),
        ]
    for copy in copies:
        copy.start()
    for copy in copies:
        copy.wait()


def final_kernel(parts, readout, out):
    share, width = out.shape
    rows = parts[...]
    context, lse = decode(rows, spread_matrix(width))
    count = rows.shape[0] // share
    cut = [slice(i * share, (i + 1) * share) for i in range(count)]
    context, _ = combine([(context[c], lse[c]) for c in cut])
    out[...] = dot(context.astype(BF16), readout[...]).astype(BF16)


def small(limit=8):
    return pltpu.CompilerParams(vmem_limit_bytes=limit * 1024 * 1024)


def on_device(history, taps, gains, up, down, w_kv, readout, queries):
    _, span, width = history.shape
    horizon, hidden = queries.shape[0], up.shape[-1]
    count = lax.axis_size("tm")
    n_pairs = count // 2
    share = horizon // count

    hist = history.reshape(span // STEP, STEP, width)
    swap = [(i, i ^ 1) for i in range(count)]
    ahead = [(2 * p + 1, 2 * p + 2) for p in range(n_pairs - 1)]
    behind = [(2 * p, 2 * p - 2) for p in range(1, n_pairs)]
    near_pairs = [(s, t + 1) for s, t in ahead] + behind
    far_pairs = ahead + [(s, t + 1) for s, t in behind]
    three = jax.ShapeDtypeStruct((3, HALF, width), BF16)
    swap_out = pl.pallas_call(
        functools.partial(pack_kernel, 0),
        out_shape=jax.ShapeDtypeStruct((4, HALF, width), BF16),
        in_specs=[HBM],
        out_specs=VMEM,
        scratch_shapes=[pltpu.SemaphoreType.DMA((1,))],
        compiler_params=small(),
        name="pack_swap",
    )(hist)
    got = lax.ppermute(swap_out, "tm", swap)
    near_out, far_out = pl.pallas_call(
        functools.partial(pack_kernel, 1),
        out_shape=[three, three],
        in_specs=[HBM],
        out_specs=[VMEM, VMEM],
        scratch_shapes=[pltpu.SemaphoreType.DMA((2,))],
        compiler_params=small(),
        name="pack_halo",
    )(hist)
    near = lax.ppermute(near_out, "tm", near_pairs)
    far = lax.ppermute(far_out, "tm", far_pairs)

    own, up_v, down_v, kv_v, readout_v = pl.pallas_call(
        functools.partial(pack_kernel, 2),
        out_shape=[jax.ShapeDtypeStruct((4, HALF, width), BF16)]
        + [jax.ShapeDtypeStruct(w.shape, w.dtype) for w in (up, down, w_kv, readout)],
        in_specs=[HBM] * 5,
        out_specs=[VMEM] * 5,
        scratch_shapes=[pltpu.SemaphoreType.DMA((5,))],
        compiler_params=small(16),
        name="stage",
    )(hist, up, down, w_kv, readout)
    state = jax.ShapeDtypeStruct((horizon, width), F32)
    per_row = 4 * width * hidden
    done = pl.pallas_call(
        own_kernel,
        out_shape=jax.ShapeDtypeStruct((2 * HALF, width), BF16),
        in_specs=[VMEM] * 5,
        out_specs=VMEM,
        compiler_params=small(16),
        cost_estimate=pl.CostEstimate(flops=2 * per_row * HALF, bytes_accessed=4 << 20, transcendentals=2 * HALF * hidden),
        name="own",
    )(own, taps, gains, up_v, down_v)
    tail, acc, top, total = pl.pallas_call(
        early_kernel,
        out_shape=[jax.ShapeDtypeStruct((4 * HALF, width), BF16), state, state, state],
        in_specs=[VMEM] * 10,
        out_specs=[VMEM] * 4,
        scratch_shapes=[
            pltpu.VMEM((9 * HALF, width), BF16)
        ],
        compiler_params=pltpu.CompilerParams(vmem_limit_bytes=32 * 1024 * 1024),
        cost_estimate=pl.CostEstimate(
            flops=(14 * per_row + 5 * 2 * per_row) * HALF, bytes_accessed=8 << 20, transcendentals=2 << 20
        ),
        name="early",
    )(own, got, near, done, taps, gains, up_v, down_v, kv_v, queries)
    lanes = width + 128
    payload = pl.pallas_call(
        late_kernel,
        out_shape=jax.ShapeDtypeStruct((horizon, lanes), BF16),
        in_specs=[VMEM] * 12,
        out_specs=VMEM,
        scratch_shapes=[
            pltpu.VMEM((7 * HALF, width), BF16), *[pltpu.VMEM(state.shape, F32)] * 3
        ],
        compiler_params=pltpu.CompilerParams(vmem_limit_bytes=32 * 1024 * 1024),
        cost_estimate=pl.CostEstimate(
            flops=(6 * per_row + 3 * 2 * per_row) * HALF, bytes_accessed=8 << 20, transcendentals=1 << 20
        ),
        name="late",
    )(own, far, tail, acc, top, total, taps, gains, up_v, down_v, kv_v, queries)
    parts = lax.all_to_all(payload, "tm", 0, 0, tiled=True)
    result = pl.pallas_call(
        final_kernel,
        out_shape=jax.ShapeDtypeStruct((share, width), BF16),
        in_specs=[VMEM] * 2,
        out_specs=VMEM,
        compiler_params=small(),
        name="final",
    )(parts, readout_v)
    return result[None]


def solution(mesh):
    placed = (P(("groups", "series"), "tm", None), P(), P(), P(), P(), P(), P(), P())
    return jax.shard_map(
        on_device,
        mesh=mesh,
        in_specs=placed,
        out_specs=P(("groups", "series"), "tm", None),
        check_vma=False,
    )
```

```python
import functools

import jax
import jax.numpy as jnp
from jax import lax
from jax.experimental import pallas as pl
from jax.experimental.pallas import tpu as pltpu
from jax.sharding import PartitionSpec as P

HEADS = 8
STEP = 256
HALF = STEP // 2
BF16, F32 = jnp.bfloat16, jnp.float32
VMEM = pl.BlockSpec(memory_space=pltpu.VMEM)
HBM = pl.BlockSpec(memory_space=pltpu.HBM)


def dot(a, b):
    return jnp.dot(a, b, preferred_element_type=F32)


def gelu(u):
    half = 0.5 * u
    return half + half * jnp.tanh(u * (0.7978845608028654 + (0.7978845608028654 * 0.044715) * (u * u)))


def groups(ref):
    return lambda g: ref[g * HALF : (g + 1) * HALF, :]


def chain(*refs):
    at = [(ref, g) for ref in refs for g in range(ref.shape[0])]
    return lambda g: at[g][0][at[g][1]]


def mix(get, first, steps, dilation, taps, gain, up, down, reach=None):
    rows, kept = [], []
    for j in range(steps):
        conv = None
        for k in range(reach[j] if reach else 3):
            value = get(first + j - k * dilation).astype(F32)
            if k == 0:
                kept.append(value)
            conv = taps[k : k + 1, :] * value if k == 0 else conv + taps[k : k + 1, :] * value
        scale = lax.rsqrt(jnp.mean(conv * conv, axis=-1, keepdims=True) + 1e-05)
        rows.append((conv * scale * gain).astype(BF16))
    inner = gelu(dot(jnp.concatenate(rows, 0), up)).astype(BF16)
    return (jnp.concatenate(kept, 0) + dot(inner, down)).astype(BF16)


def attend(x2, w_kv, queries, absent=None):
    pairs = dot(x2, w_kv).astype(BF16)
    horizon, width = queries.shape
    low = lax.broadcasted_iota(jnp.int32, (horizon, 128), 1) < 64
    zero = jnp.zeros((horizon, 128), BF16)
    acc, top, total, scores = [], [], [], []
    for p in range(width // 128):
        lanes = slice(128 * p, 128 * p + 128)
        q = queries[:, lanes] * jnp.asarray(0.125, BF16)
        q2 = jnp.concatenate([jnp.where(low, q, zero), jnp.where(low, zero, q)], 0)
        scores.append(
            lax.dot_general(q2, pairs[:, lanes], (((1,), (1,)), ((), ())), preferred_element_type=F32)
        )
    if absent is not None:
        row = lax.broadcasted_iota(jnp.int32, (1, x2.shape[0]), 1)
        bias = jnp.where(row < absent, 0.0, -1e30).astype(F32)
        scores = [s + bias for s in scores]
    for p in range(width // 128):
        m = jnp.max(scores[p], axis=-1, keepdims=True)
        e = jnp.exp(scores[p] - m)
        s = jnp.sum(e, axis=-1, keepdims=True)
        c = dot(e.astype(BF16), pairs[:, width + 128 * p : width + 128 * p + 128])
        acc.append(jnp.where(low, c[:horizon], c[horizon:]))
        top.append(jnp.where(low, m[:horizon], m[horizon:]))
        total.append(jnp.where(low, s[:horizon], s[horizon:]))
    return jnp.concatenate(acc, 1), jnp.concatenate(top, 1), jnp.concatenate(total, 1)


def encode(context, lse):
    lane = lax.broadcasted_iota(jnp.int32, (lse.shape[0], 128), 1) & 63
    stats = jnp.zeros((lse.shape[0], 128), F32)
    for p in range(lse.shape[1] // 128):
        rest = lse[:, 128 * p : 128 * p + 128]
        for piece in range(3):
            part = rest.astype(BF16).astype(F32)
            stats = jnp.where(lane == 3 * p + piece, part, stats)
            rest = rest - part
    return jnp.concatenate([context.astype(BF16), stats.astype(BF16)], 1)


def spread_matrix(width):
    row = lax.broadcasted_iota(jnp.int32, (128, width), 0)
    col = lax.broadcasted_iota(jnp.int32, (128, width), 1)
    piece = (row & 63) - 3 * (col >> 7)
    return jnp.where((piece >= 0) & (piece < 3) & ((row >> 6) == ((col >> 6) & 1)), 1.0, 0.0).astype(BF16)


def decode(rows, spread):
    width = rows.shape[1] - 128
    return rows[:, :width].astype(F32), dot(rows[:, width:], spread)


def combine(parts):
    top = functools.reduce(jnp.maximum, [l for _, l in parts])
    weights = [jnp.exp(l - top) for _, l in parts]
    total = functools.reduce(jnp.add, weights)
    context = functools.reduce(jnp.add, [w * c for w, (c, _) in zip(weights, parts)])
    return context / total, top + jnp.log(total)


def join(a, b):
    best = jnp.maximum(a[1], b[1])
    wa, wb = jnp.exp(a[1] - best), jnp.exp(b[1] - best)
    return a[0] * wa + b[0] * wb, best, a[2] * wa + b[2] * wb


def first_steps(x1, taps, gains, up_v, down_v, kv_v, queries, state):
    x2 = mix(groups(x1), 1, 3, 2, taps[1], gains[1:2, :], up_v[1], down_v[1], (1, 1, 2))
    added = join([ref[...] for ref in state], attend(x2, kv_v[...], queries[...]))
    for ref, value in zip(state, added):
        ref[...] = value


def own_kernel(own, taps, gains, up_v, down_v, out):
    out[...] = mix(chain(own), 2, 2, 1, taps[0], gains[0:1, :], up_v[0], down_v[0])


def early_kernel(own, got, near, done, taps, gains, up_v, down_v, kv_v, queries, tail, acc, top, total, x1):
    here, count = lax.axis_index("tm"), lax.axis_size("tm")

    def block_one(refs, first, done_at, tail_at):
        x1[done_at * HALF : (done_at + 2) * HALF, :] = done[...]
        x1[first * HALF : (first + 7) * HALF, :] = mix(
            chain(*refs), first + 2, 7, 1, taps[0], gains[0:1, :], up_v[0], down_v[0]
        )
        tail[...] = x1[tail_at * HALF : (tail_at + 4) * HALF, :]

    @pl.when(lax.rem(here, 2) == 0)
    def _():
        block_one((own, got, near), 2, 0, 0)

    @pl.when(lax.rem(here, 2) == 1)
    def _():
        block_one((near, got, own), 0, 7, 5)

    x2 = mix(groups(x1), 4, 5, 2, taps[1], gains[1:2, :], up_v[1], down_v[1])
    absent = jnp.where(here == count - 2, 2 * HALF, 5 * HALF)
    acc[...], top[...], total[...] = attend(x2, kv_v[...], queries[...], absent)

    @pl.when(here == 1)
    def _():
        first_steps(x1, taps, gains, up_v, down_v, kv_v, queries, (acc, top, total))


def late_kernel(own, far, tail, acc, top, total, taps, gains, up_v, down_v, kv_v, queries, out, x1, acc2, top2, total2):
    here, count = lax.axis_index("tm"), lax.axis_size("tm")

    def block_one(refs, new_at, tail_at):
        x1[tail_at * HALF : (tail_at + 4) * HALF, :] = tail[...]
        x1[new_at * HALF : (new_at + 3) * HALF, :] = mix(
            chain(*refs), 2, 3, 1, taps[0], gains[0:1, :], up_v[0], down_v[0]
        )

    @pl.when(lax.rem(here, 2) == 0)
    def _():
        block_one((far, own.at[0:2]), 0, 3)

    @pl.when(lax.rem(here, 2) == 1)
    def _():
        block_one((own.at[2:4], far), 4, 0)

    x2 = mix(groups(x1), 4, 3, 2, taps[1], gains[1:2, :], up_v[1], down_v[1])
    absent = jnp.where(here == count - 1, 0, 3 * HALF)
    acc2[...], top2[...], total2[...] = join(
        (acc[...], top[...], total[...]), attend(x2, kv_v[...], queries[...], absent)
    )

    @pl.when(here == 0)
    def _():
        first_steps(x1, taps, gains, up_v, down_v, kv_v, queries, (acc2, top2, total2))

    out[...] = encode(acc2[...] / total2[...], top2[...] + jnp.log(total2[...]))


def pack_kernel(n, hist, *refs):
    side = lax.rem(lax.axis_index("tm"), 2)
    mine = pl.ds(pl.multiple_of(side * HALF, HALF), HALF)
    other = pl.ds(pl.multiple_of((1 - side) * HALF, HALF), HALF)
    three = pl.ds(side, 3)
    if n == 0:
        swap_out, sem = refs
        copies = [pltpu.make_async_copy(hist.at[:, other, :], swap_out, sem.at[0])]
    elif n == 2:
        whole, (own_out, *outs, sem) = refs[:4], refs[4:]
        copies = [
            pltpu.make_async_copy(a, b, sem.at[i]) for i, (a, b) in enumerate(zip(whole, outs))
        ] + [pltpu.make_async_copy(hist.at[:, mine, :], own_out, sem.at[4])]
    else:
        near_out, far_out, sem = refs
        copies = [
            pltpu.make_async_copy(hist.at[three, mine, :], near_out, sem.at[0]),
            pltpu.make_async_copy(hist.at[three, other, :], far_out, sem.at[1]),
        ]
    for copy in copies:
        copy.start()
    for copy in copies:
        copy.wait()


def final_kernel(parts, readout, out):
    share, width = out.shape
    rows = parts[...]
    context, lse = decode(rows, spread_matrix(width))
    count = rows.shape[0] // share
    cut = [slice(i * share, (i + 1) * share) for i in range(count)]
    context, _ = combine([(context[c], lse[c]) for c in cut])
    out[...] = dot(context.astype(BF16), readout[...]).astype(BF16)


def small(limit=8):
    return pltpu.CompilerParams(vmem_limit_bytes=limit * 1024 * 1024)


def on_device(history, taps, gains, up, down, w_kv, readout, queries):
    _, span, width = history.shape
    horizon, hidden = queries.shape[0], up.shape[-1]
    count = lax.axis_size("tm")
    n_pairs = count // 2
    share = horizon // count

    hist = history.reshape(span // STEP, STEP, width)
    swap = [(i, i ^ 1) for i in range(count)]
    ahead = [(2 * p + 1, 2 * p + 2) for p in range(n_pairs - 1)]
    behind = [(2 * p, 2 * p - 2) for p in range(1, n_pairs)]
    near_pairs = [(s, t + 1) for s, t in ahead] + behind
    far_pairs = ahead + [(s, t + 1) for s, t in behind]
    three = jax.ShapeDtypeStruct((3, HALF, width), BF16)
    swap_out = pl.pallas_call(
        functools.partial(pack_kernel, 0),
        out_shape=jax.ShapeDtypeStruct((4, HALF, width), BF16),
        in_specs=[HBM],
        out_specs=VMEM,
        scratch_shapes=[pltpu.SemaphoreType.DMA((1,))],
        compiler_params=small(),
        name="pack_swap",
    )(hist)
    got = lax.ppermute(swap_out, "tm", swap)
    near_out, far_out = pl.pallas_call(
        functools.partial(pack_kernel, 1),
        out_shape=[three, three],
        in_specs=[HBM],
        out_specs=[VMEM, VMEM],
        scratch_shapes=[pltpu.SemaphoreType.DMA((2,))],
        compiler_params=small(),
        name="pack_halo",
    )(hist)
    near = lax.ppermute(near_out, "tm", near_pairs)
    far = lax.ppermute(far_out, "tm", far_pairs)

    own, up_v, down_v, kv_v, readout_v = pl.pallas_call(
        functools.partial(pack_kernel, 2),
        out_shape=[jax.ShapeDtypeStruct((4, HALF, width), BF16)]
        + [jax.ShapeDtypeStruct(w.shape, w.dtype) for w in (up, down, w_kv, readout)],
        in_specs=[HBM] * 5,
        out_specs=[VMEM] * 5,
        scratch_shapes=[pltpu.SemaphoreType.DMA((5,))],
        compiler_params=small(16),
        name="stage",
    )(hist, up, down, w_kv, readout)
    state = jax.ShapeDtypeStruct((horizon, width), F32)
    per_row = 4 * width * hidden
    done = pl.pallas_call(
        own_kernel,
        out_shape=jax.ShapeDtypeStruct((2 * HALF, width), BF16),
        in_specs=[VMEM] * 5,
        out_specs=VMEM,
        compiler_params=small(16),
        cost_estimate=pl.CostEstimate(flops=2 * per_row * HALF, bytes_accessed=4 << 20, transcendentals=2 * HALF * hidden),
        name="own",
    )(own, taps, gains, up_v, down_v)
    tail, acc, top, total = pl.pallas_call(
        early_kernel,
        out_shape=[jax.ShapeDtypeStruct((4 * HALF, width), BF16), state, state, state],
        in_specs=[VMEM] * 10,
        out_specs=[VMEM] * 4,
        scratch_shapes=[
            pltpu.VMEM((9 * HALF, width), BF16)
        ],
        compiler_params=pltpu.CompilerParams(vmem_limit_bytes=32 * 1024 * 1024),
        cost_estimate=pl.CostEstimate(
            flops=(14 * per_row + 5 * 2 * per_row) * HALF, bytes_accessed=8 << 20, transcendentals=2 << 20
        ),
        name="early",
    )(own, got, near, done, taps, gains, up_v, down_v, kv_v, queries)
    lanes = width + 128
    payload = pl.pallas_call(
        late_kernel,
        out_shape=jax.ShapeDtypeStruct((horizon, lanes), BF16),
        in_specs=[VMEM] * 12,
        out_specs=VMEM,
        scratch_shapes=[
            pltpu.VMEM((7 * HALF, width), BF16), *[pltpu.VMEM(state.shape, F32)] * 3
        ],
        compiler_params=pltpu.CompilerParams(vmem_limit_bytes=32 * 1024 * 1024),
        cost_estimate=pl.CostEstimate(
            flops=(6 * per_row + 3 * 2 * per_row) * HALF, bytes_accessed=8 << 20, transcendentals=1 << 20
        ),
        name="late",
    )(own, far, tail, acc, top, total, taps, gains, up_v, down_v, kv_v, queries)
    parts = lax.all_to_all(payload, "tm", 0, 0, tiled=True)
    result = pl.pallas_call(
        final_kernel,
        out_shape=jax.ShapeDtypeStruct((share, width), BF16),
        in_specs=[VMEM] * 2,
        out_specs=VMEM,
        compiler_params=small(),
        name="final",
    )(parts, readout_v)
    return result[None]


def solution(mesh):
    placed = (P(("groups", "series"), "tm", None), P(), P(), P(), P(), P(), P(), P())
    return jax.shard_map(
        on_device,
        mesh=mesh,
        in_specs=placed,
        out_specs=P(("groups", "series"), "tm", None),
        check_vma=False,
    )
```

```python
import functools

import jax
import jax.numpy as jnp
from jax import lax
from jax.experimental import pallas as pl
from jax.experimental.pallas import tpu as pltpu
from jax.sharding import PartitionSpec as P

HEADS = 8
STEP = 256
HALF = STEP // 2
BF16, F32 = jnp.bfloat16, jnp.float32
VMEM = pl.BlockSpec(memory_space=pltpu.VMEM)
HBM = pl.BlockSpec(memory_space=pltpu.HBM)


def dot(a, b):
    return jnp.dot(a, b, preferred_element_type=F32)


def gelu(u):
    half = 0.5 * u
    return half + half * jnp.tanh(u * (0.7978845608028654 + (0.7978845608028654 * 0.044715) * (u * u)))


def groups(ref):
    return lambda g: ref[g * HALF : (g + 1) * HALF, :]


def chain(*refs):
    at = [(ref, g) for ref in refs for g in range(ref.shape[0])]
    return lambda g: at[g][0][at[g][1]]


def mix(get, first, steps, dilation, taps, gain, up, down, reach=None):
    rows, kept = [], []
    for j in range(steps):
        conv = None
        for k in range(reach[j] if reach else 3):
            value = get(first + j - k * dilation).astype(F32)
            if k == 0:
                kept.append(value)
            conv = taps[k : k + 1, :] * value if k == 0 else conv + taps[k : k + 1, :] * value
        scale = lax.rsqrt(jnp.mean(conv * conv, axis=-1, keepdims=True) + 1e-05)
        rows.append((conv * scale * gain).astype(BF16))
    inner = gelu(dot(jnp.concatenate(rows, 0), up)).astype(BF16)
    return (jnp.concatenate(kept, 0) + dot(inner, down)).astype(BF16)


def attend(x2, w_kv, queries, absent=None):
    pairs = dot(x2, w_kv).astype(BF16)
    horizon, width = queries.shape
    low = lax.broadcasted_iota(jnp.int32, (horizon, 128), 1) < 64
    zero = jnp.zeros((horizon, 128), BF16)
    acc, top, total, scores = [], [], [], []
    for p in range(width // 128):
        lanes = slice(128 * p, 128 * p + 128)
        q = queries[:, lanes] * jnp.asarray(0.125, BF16)
        q2 = jnp.concatenate([jnp.where(low, q, zero), jnp.where(low, zero, q)], 0)
        scores.append(
            lax.dot_general(q2, pairs[:, lanes], (((1,), (1,)), ((), ())), preferred_element_type=F32)
        )
    if absent is not None:
        row = lax.broadcasted_iota(jnp.int32, (1, x2.shape[0]), 1)
        bias = jnp.where(row < absent, 0.0, -1e30).astype(F32)
        scores = [s + bias for s in scores]
    for p in range(width // 128):
        m = jnp.max(scores[p], axis=-1, keepdims=True)
        e = jnp.exp(scores[p] - m)
        s = jnp.sum(e, axis=-1, keepdims=True)
        c = dot(e.astype(BF16), pairs[:, width + 128 * p : width + 128 * p + 128])
        acc.append(jnp.where(low, c[:horizon], c[horizon:]))
        top.append(jnp.where(low, m[:horizon], m[horizon:]))
        total.append(jnp.where(low, s[:horizon], s[horizon:]))
    return jnp.concatenate(acc, 1), jnp.concatenate(top, 1), jnp.concatenate(total, 1)


def encode(context, lse):
    lane = lax.broadcasted_iota(jnp.int32, (lse.shape[0], 128), 1) & 63
    stats = jnp.zeros((lse.shape[0], 128), F32)
    for p in range(lse.shape[1] // 128):
        rest = lse[:, 128 * p : 128 * p + 128]
        for piece in range(3):
            part = rest.astype(BF16).astype(F32)
            stats = jnp.where(lane == 3 * p + piece, part, stats)
            rest = rest - part
    return jnp.concatenate([context.astype(BF16), stats.astype(BF16)], 1)


def spread_matrix(width):
    row = lax.broadcasted_iota(jnp.int32, (128, width), 0)
    col = lax.broadcasted_iota(jnp.int32, (128, width), 1)
    piece = (row & 63) - 3 * (col >> 7)
    return jnp.where((piece >= 0) & (piece < 3) & ((row >> 6) == ((col >> 6) & 1)), 1.0, 0.0).astype(BF16)


def decode(rows, spread):
    width = rows.shape[1] - 128
    return rows[:, :width].astype(F32), dot(rows[:, width:], spread)


def combine(parts):
    top = functools.reduce(jnp.maximum, [l for _, l in parts])
    weights = [jnp.exp(l - top) for _, l in parts]
    total = functools.reduce(jnp.add, weights)
    context = functools.reduce(jnp.add, [w * c for w, (c, _) in zip(weights, parts)])
    return context / total, top + jnp.log(total)


def join(a, b):
    best = jnp.maximum(a[1], b[1])
    wa, wb = jnp.exp(a[1] - best), jnp.exp(b[1] - best)
    return a[0] * wa + b[0] * wb, best, a[2] * wa + b[2] * wb


def first_steps(x1, taps, gains, up_v, down_v, kv_v, queries, state):
    x2 = mix(groups(x1), 1, 3, 2, taps[1], gains[1:2, :], up_v[1], down_v[1], (1, 1, 2))
    added = join([ref[...] for ref in state], attend(x2, kv_v[...], queries[...]))
    for ref, value in zip(state, added):
        ref[...] = value


def own_kernel(own, taps, gains, up_v, down_v, out):
    out[...] = mix(chain(own), 2, 2, 1, taps[0], gains[0:1, :], up_v[0], down_v[0])


def early_kernel(own, got, near, done, taps, gains, up_v, down_v, kv_v, queries, tail, acc, top, total, x1):
    here, count = lax.axis_index("tm"), lax.axis_size("tm")

    def block_one(refs, first, done_at, tail_at):
        x1[done_at * HALF : (done_at + 2) * HALF, :] = done[...]
        x1[first * HALF : (first + 7) * HALF, :] = mix(
            chain(*refs), first + 2, 7, 1, taps[0], gains[0:1, :], up_v[0], down_v[0]
        )
        tail[...] = x1[tail_at * HALF : (tail_at + 4) * HALF, :]

    @pl.when(lax.rem(here, 2) == 0)
    def _():
        block_one((own, got, near), 2, 0, 0)

    @pl.when(lax.rem(here, 2) == 1)
    def _():
        block_one((near, got, own), 0, 7, 5)

    x2 = mix(groups(x1), 4, 5, 2, taps[1], gains[1:2, :], up_v[1], down_v[1])
    absent = jnp.where(here == count - 2, 2 * HALF, 5 * HALF)
    acc[...], top[...], total[...] = attend(x2, kv_v[...], queries[...], absent)

    @pl.when(here == 1)
    def _():
        first_steps(x1, taps, gains, up_v, down_v, kv_v, queries, (acc, top, total))


def late_kernel(own, far, tail, acc, top, total, taps, gains, up_v, down_v, kv_v, queries, out, x1, acc2, top2, total2):
    here, count = lax.axis_index("tm"), lax.axis_size("tm")

    def block_one(refs, new_at, tail_at):
        x1[tail_at * HALF : (tail_at + 4) * HALF, :] = tail[...]
        x1[new_at * HALF : (new_at + 3) * HALF, :] = mix(
            chain(*refs), 2, 3, 1, taps[0], gains[0:1, :], up_v[0], down_v[0]
        )

    @pl.when(lax.rem(here, 2) == 0)
    def _():
        block_one((far, own.at[0:2]), 0, 3)

    @pl.when(lax.rem(here, 2) == 1)
    def _():
        block_one((own.at[2:4], far), 4, 0)

    x2 = mix(groups(x1), 4, 3, 2, taps[1], gains[1:2, :], up_v[1], down_v[1])
    absent = jnp.where(here == count - 1, 0, 3 * HALF)
    acc2[...], top2[...], total2[...] = join(
        (acc[...], top[...], total[...]), attend(x2, kv_v[...], queries[...], absent)
    )

    @pl.when(here == 0)
    def _():
        first_steps(x1, taps, gains, up_v, down_v, kv_v, queries, (acc2, top2, total2))

    out[...] = encode(acc2[...] / total2[...], top2[...] + jnp.log(total2[...]))


def pack_kernel(n, hist, *refs):
    side = lax.rem(lax.axis_index("tm"), 2)
    mine = pl.ds(pl.multiple_of(side * HALF, HALF), HALF)
    other = pl.ds(pl.multiple_of((1 - side) * HALF, HALF), HALF)
    three = pl.ds(side, 3)
    if n == 0:
        swap_out, sem = refs
        copies = [pltpu.make_async_copy(hist.at[:, other, :], swap_out, sem.at[0])]
    elif n == 2:
        whole, (own_out, *outs, sem) = refs[:4], refs[4:]
        copies = [
            pltpu.make_async_copy(a, b, sem.at[i]) for i, (a, b) in enumerate(zip(whole, outs))
        ] + [pltpu.make_async_copy(hist.at[:, mine, :], own_out, sem.at[4])]
    else:
        near_out, far_out, sem = refs
        copies = [
            pltpu.make_async_copy(hist.at[three, mine, :], near_out, sem.at[0]),
            pltpu.make_async_copy(hist.at[three, other, :], far_out, sem.at[1]),
        ]
    for copy in copies:
        copy.start()
    for copy in copies:
        copy.wait()


def final_kernel(parts, readout, out):
    share, width = out.shape
    rows = parts[...]
    context, lse = decode(rows, spread_matrix(width))
    count = rows.shape[0] // share
    cut = [slice(i * share, (i + 1) * share) for i in range(count)]
    context, _ = combine([(context[c], lse[c]) for c in cut])
    out[...] = dot(context.astype(BF16), readout[...]).astype(BF16)


def small(limit=8):
    return pltpu.CompilerParams(vmem_limit_bytes=limit * 1024 * 1024)


def on_device(history, taps, gains, up, down, w_kv, readout, queries):
    _, span, width = history.shape
    horizon, hidden = queries.shape[0], up.shape[-1]
    count = lax.axis_size("tm")
    n_pairs = count // 2
    share = horizon // count

    hist = history.reshape(span // STEP, STEP, width)
    swap = [(i, i ^ 1) for i in range(count)]
    ahead = [(2 * p + 1, 2 * p + 2) for p in range(n_pairs - 1)]
    behind = [(2 * p, 2 * p - 2) for p in range(1, n_pairs)]
    near_pairs = [(s, t + 1) for s, t in ahead] + behind
    far_pairs = ahead + [(s, t + 1) for s, t in behind]
    three = jax.ShapeDtypeStruct((3, HALF, width), BF16)
    swap_out = pl.pallas_call(
        functools.partial(pack_kernel, 0),
        out_shape=jax.ShapeDtypeStruct((4, HALF, width), BF16),
        in_specs=[HBM],
        out_specs=VMEM,
        scratch_shapes=[pltpu.SemaphoreType.DMA((1,))],
        compiler_params=small(),
        name="pack_swap",
    )(pltpu.with_memory_space_constraint(hist, pltpu.HBM))
    got = lax.ppermute(swap_out, "tm", swap)
    near_out, far_out = pl.pallas_call(
        functools.partial(pack_kernel, 1),
        out_shape=[three, three],
        in_specs=[HBM],
        out_specs=[VMEM, VMEM],
        scratch_shapes=[pltpu.SemaphoreType.DMA((2,))],
        compiler_params=small(),
        name="pack_halo",
    )(hist)
    near = lax.ppermute(near_out, "tm", near_pairs)
    far = lax.ppermute(far_out, "tm", far_pairs)

    own, up_v, down_v, kv_v, readout_v = pl.pallas_call(
        functools.partial(pack_kernel, 2),
        out_shape=[jax.ShapeDtypeStruct((4, HALF, width), BF16)]
        + [jax.ShapeDtypeStruct(w.shape, w.dtype) for w in (up, down, w_kv, readout)],
        in_specs=[HBM] * 5,
        out_specs=[VMEM] * 5,
        scratch_shapes=[pltpu.SemaphoreType.DMA((5,))],
        compiler_params=small(16),
        name="stage",
    )(hist, up, down, w_kv, readout)
    state = jax.ShapeDtypeStruct((horizon, width), F32)
    per_row = 4 * width * hidden
    done = pl.pallas_call(
        own_kernel,
        out_shape=jax.ShapeDtypeStruct((2 * HALF, width), BF16),
        in_specs=[VMEM] * 5,
        out_specs=VMEM,
        compiler_params=small(16),
        cost_estimate=pl.CostEstimate(flops=2 * per_row * HALF, bytes_accessed=4 << 20, transcendentals=2 * HALF * hidden),
        name="own",
    )(own, taps, gains, up_v, down_v)
    tail, acc, top, total = pl.pallas_call(
        early_kernel,
        out_shape=[jax.ShapeDtypeStruct((4 * HALF, width), BF16), state, state, state],
        in_specs=[VMEM] * 10,
        out_specs=[VMEM] * 4,
        scratch_shapes=[
            pltpu.VMEM((9 * HALF, width), BF16)
        ],
        compiler_params=pltpu.CompilerParams(vmem_limit_bytes=32 * 1024 * 1024),
        cost_estimate=pl.CostEstimate(
            flops=(14 * per_row + 5 * 2 * per_row) * HALF, bytes_accessed=8 << 20, transcendentals=2 << 20
        ),
        name="early",
    )(own, got, near, done, taps, gains, up_v, down_v, kv_v, queries)
    lanes = width + 128
    payload = pl.pallas_call(
        late_kernel,
        out_shape=jax.ShapeDtypeStruct((horizon, lanes), BF16),
        in_specs=[VMEM] * 12,
        out_specs=VMEM,
        scratch_shapes=[
            pltpu.VMEM((7 * HALF, width), BF16), *[pltpu.VMEM(state.shape, F32)] * 3
        ],
        compiler_params=pltpu.CompilerParams(vmem_limit_bytes=32 * 1024 * 1024),
        cost_estimate=pl.CostEstimate(
            flops=(6 * per_row + 3 * 2 * per_row) * HALF, bytes_accessed=8 << 20, transcendentals=1 << 20
        ),
        name="late",
    )(own, far, tail, acc, top, total, taps, gains, up_v, down_v, kv_v, queries)
    parts = lax.all_to_all(payload, "tm", 0, 0, tiled=True)
    result = pl.pallas_call(
        final_kernel,
        out_shape=jax.ShapeDtypeStruct((share, width), BF16),
        in_specs=[VMEM] * 2,
        out_specs=VMEM,
        compiler_params=small(),
        name="final",
    )(parts, readout_v)
    return result[None]


def solution(mesh):
    placed = (P(("groups", "series"), "tm", None), P(), P(), P(), P(), P(), P(), P())
    return jax.shard_map(
        on_device,
        mesh=mesh,
        in_specs=placed,
        out_specs=P(("groups", "series"), "tm", None),
        check_vma=False,
    )
```
